512 devices in a mesh: rep: 64 (over z, y), tp: 8 (over x, core).
Axes of the slice: x: 4, y: 8, z: 8, core: 2. Of those that a mesh axis runs over, the one named last changes fastest.
Arguments:
- suffix: bfloat16 [8192, 10240], P(('rep', 'tp')), may hold values from -5 to 5
- key_value_pages: bfloat16 [2, 384, 128, 1024], P(None, 'rep', None, 'tp'), may hold values from -5 to 5
- placement: int32 [64], replicated, may hold values from 0 to 63, each once
- lengths: int32 [64], replicated, may hold values from 1 to 384, 8192 in all
- page_table: int32 [64, 4], P('rep'), may hold values from 0 to 5, as said below
Outputs:
- attended: bfloat16 [8192, 8192], P(('rep', 'tp'))
The draws below stay inside these ranges and needn't reach their ends.
Inputs may be any that keep to these rules, and one draw needn't show every extreme that they name: `placement`: each group holds the prefix of exactly one request. The lengths sum to 8192 and the longest is exactly 384. `page_table`: row g names 4 different pages of group g's own pool.
All inputs are finite; a program needn't handle non-finite values.
Results may differ from the reference program's by a relative error of at most 0.0046.
Values may be sent and summed in bfloat16 or wider, within the bound.
A program may use at most 64 MiB of HBM per device.

```python
import math
import jax
import jax.numpy as jnp
import numpy as np
from jax import lax

QUERY_HEADS = 64
KEY_VALUE_HEADS = 8
HEAD_SIZE = 128
PAGE_TOKENS = 128
TOK_DEV = 16
PREFIX_TOKENS = 512
PAGES = 4
POOL = 6
TOTAL_PAGES = 384
TOKENS = 8192
SUFFIX_LENGTH = 384
N_REP = 64
N_TP = 8


def draw_suffix(key, part):
    key = jax.random.fold_in(key, 11)
    key_base = jax.random.fold_in(key, 0)
    column_index = (QUERY_HEADS + 2 * KEY_VALUE_HEADS) * HEAD_SIZE
    value_rows = jnp.clip(jax.random.normal(key_base, (TOKENS, column_index), jnp.float32), -5.0, 5.0)
    return value_rows.astype(jnp.bfloat16)


def draw_key_value_pages(key, part):
    key = jax.random.fold_in(key, 7)
    value_rows = jnp.clip(jax.random.normal(key, (2, TOTAL_PAGES, PAGE_TOKENS, KEY_VALUE_HEADS * HEAD_SIZE), jnp.float32), -5.0, 5.0)
    return value_rows.astype(jnp.bfloat16)


def draw_page_table(key, part):
    key = jax.random.fold_in(key, 5)
    group_keys = jax.random.split(key, N_REP)
    tables = jax.vmap(lambda single: jax.random.permutation(single, POOL)[:PAGES])(group_keys)
    return tables.astype(jnp.int32)


def profile(number_of, total, limit, slope):
    loads = [(1 << 20) // math.isqrt(rank ** slope) + 1 for rank in range(2, number_of + 1)]
    rest, counts = total - limit - (number_of - 1), [1] * (number_of - 1)
    while rest > 0:
        movable = [i for i in range(number_of - 1) if counts[i] < limit]
        pool, left = sum([loads[i] for i in movable]), rest
        for i in movable:
            addition = min(limit - counts[i], max(1, left * loads[i] // pool), rest)
            counts[i] = counts[i] + addition
            rest = rest - addition
    return np.array([limit] + counts)


def uneven_parts(rng, amount, total, limit, slope):
    if amount == 2:
        one = jax.random.randint(rng, (), max(1, total - limit), min(limit, total - 1) + 1)
        return jnp.stack([one, total - one])
    tallies = jnp.asarray(profile(amount, total, limit, slope), jnp.int32)
    twos = (amount - 1) // 2
    donor, sink = tallies[1:1 + 2 * twos:2], tallies[2:2 + 2 * twos:2]
    room = jnp.minimum(donor - 1, limit - sink)
    moved = jax.random.randint(jax.random.fold_in(rng, 1), (twos,), 0, 1 << 20) % (room + 1)
    tallies = tallies.at[1:1 + 2 * twos:2].set(donor - moved).at[2:2 + 2 * twos:2].set(sink + moved)
    return tallies[jax.random.permutation(jax.random.fold_in(rng, 2), amount)]


def setup_inputs(seed: int = 0) -> dict:
    streams_of = jax.random.split(jax.random.key(seed), 6)
    return {
        "suffix": draw_suffix(jax.random.fold_in(streams_of[5], 71), 0),
        "key_value_pages": draw_key_value_pages(jax.random.fold_in(streams_of[5], 71), 0),
        "placement": jax.random.permutation(streams_of[2], N_REP).astype(jnp.int32),
        "lengths": uneven_parts(streams_of[3], N_REP, TOKENS, SUFFIX_LENGTH, 2).astype(jnp.int32),
        "page_table": draw_page_table(jax.random.fold_in(streams_of[5], 71), 0),
    }


def reference(suffix, key_value_pages, placement, lengths, page_table):
    devices_all = N_REP * N_TP
    group_width = QUERY_HEADS // KEY_VALUE_HEADS
    block = math.gcd(128, SUFFIX_LENGTH)
    scale = 1.0 / math.sqrt(HEAD_SIZE)
    ends_at = jnp.cumsum(lengths).astype(jnp.int32)
    starts_at = (ends_at - lengths).astype(jnp.int32)
    key_position = jnp.concatenate([jnp.full((PREFIX_TOKENS,), -1, jnp.int32), jnp.arange(SUFFIX_LENGTH, dtype=jnp.int32)])

    def per_request(request, output):
        group = placement[request]
        first_pos = starts_at[request]
        count = lengths[request]
        page_pool_rows = (group * POOL + page_table[group]).astype(jnp.int32)
        paged_rows = jnp.take(key_value_pages, page_pool_rows, axis=1).reshape(2, PREFIX_TOKENS, KEY_VALUE_HEADS, HEAD_SIZE)
        offsets = jnp.arange(SUFFIX_LENGTH, dtype=jnp.int32)
        live = offsets < count
        order_index = first_pos + offsets
        anchor = jnp.where(live, order_index % devices_all * TOK_DEV + order_index // devices_all, 0).astype(jnp.int32)
        token_matrix = jnp.take(suffix, anchor, axis=0)
        query_rows = token_matrix[:, :QUERY_HEADS * HEAD_SIZE].reshape(SUFFIX_LENGTH, KEY_VALUE_HEADS, group_width, HEAD_SIZE)
        suffix_key_rows = token_matrix[:, QUERY_HEADS * HEAD_SIZE:(QUERY_HEADS + KEY_VALUE_HEADS) * HEAD_SIZE].reshape(SUFFIX_LENGTH, KEY_VALUE_HEADS, HEAD_SIZE)
        suffix_value_rows = token_matrix[:, (QUERY_HEADS + KEY_VALUE_HEADS) * HEAD_SIZE:].reshape(SUFFIX_LENGTH, KEY_VALUE_HEADS, HEAD_SIZE)
        keys_all = jnp.concatenate([paged_rows[0], suffix_key_rows], axis=0).astype(jnp.float32)
        vals_all = jnp.concatenate([paged_rows[1], suffix_value_rows], axis=0).astype(jnp.float32)
        key_valid = jnp.concatenate([jnp.ones((PREFIX_TOKENS,), bool), live])
        destination = jnp.where(live, anchor, TOKENS).astype(jnp.int32)

        def per_block(index, carried):
            start = (index * block).astype(jnp.int32)
            query_block = lax.dynamic_slice_in_dim(query_rows, start, block, 0).astype(jnp.float32)
            query_position = start + jnp.arange(block, dtype=jnp.int32)
            visible = key_valid[None, :] & (key_position[None, :] <= query_position[:, None])
            scores = jnp.einsum('qkgd,nkd->kgqn', query_block, keys_all) * scale
            scores = jnp.where(visible[None, None], scores, -jnp.inf)
            highest = lax.optimization_barrier(jnp.max(scores, axis=-1, keepdims=True))
            expo = jnp.exp(scores - highest)
            total = lax.optimization_barrier(jnp.sum(expo, axis=-1, keepdims=True))
            rounded = lax.optimization_barrier(expo.astype(jnp.bfloat16))
            weights = rounded.astype(jnp.float32)
            mixed = jnp.einsum('kgqn,nkd->kgqd', weights, vals_all) / total
            mixed = mixed.transpose(2, 0, 1, 3).reshape(block, QUERY_HEADS * HEAD_SIZE).astype(jnp.bfloat16)
            rows_to = lax.dynamic_slice_in_dim(destination, start, block, 0)
            return carried.at[rows_to].set(mixed, mode='drop')
        blocks_needed = (count + block - 1) // block
        return lax.fori_loop(0, blocks_needed, per_block, output)
    output = jnp.zeros((TOKENS, QUERY_HEADS * HEAD_SIZE), jnp.bfloat16)
    return lax.fori_loop(0, N_REP, per_request, output)
```

```python
import functools
import math

import jax
import jax.numpy as jnp
from jax import lax
from jax.experimental import pallas as pl
from jax.experimental.pallas import tpu as pltpu
from jax.sharding import PartitionSpec as P

QUERY_HEADS = 64
KEY_VALUE_HEADS = 8
HEAD = 128
REPS = 64
TPS = 8
ROUNDS = 16
DEVICES = REPS * TPS
GROUP_HEADS = QUERY_HEADS // TPS
PARTS = GROUP_HEADS // 2
KV = PARTS
PREFIX = 512
BLOCK = 128
MESH = pl.DeviceIdType.MESH
F32 = jnp.float32
I32 = jnp.int32
BF16 = jnp.bfloat16


def iota(shape, dim):
    return lax.broadcasted_iota(I32, shape, dim)


def kernel(
    suffix, pages, place_row, place_col, len_row, len_col, table, out,
    rows_in, pool, pick, place, keys, vals, sent, got, ans, back, rows_out,
    pool_sem, x_send, x_recv, x_own, f_send, f_recv, f_own, b_send, b_recv, b_own, o_send, o_recv, o_own,
):
    rep = lax.axis_index("rep")
    tp = lax.axis_index("tp")
    z, y = rep // 8, lax.rem(rep, 8)

    def peer(step):
        a, b = step // 8, lax.rem(step, 8)
        return lax.rem(z + lax.rem(a + b, 8), 8) * 8 + lax.rem(y + b, 8)

    pool_copy = pltpu.make_async_copy(pages, pool, pool_sem)
    pool_copy.start()

    barrier = pltpu.get_barrier_semaphore()

    @pl.loop(1, TPS)
    def _(step):
        pl.semaphore_signal(
            barrier, inc=1, device_id=(rep, lax.rem(tp + step, TPS)), device_id_type=MESH
        )

    @pl.loop(1, REPS)
    def _(step):
        pl.semaphore_signal(barrier, inc=1, device_id=(peer(step), tp), device_id_type=MESH)

    lens_r = len_row[...].astype(F32)
    lens_c = len_col[...].astype(F32)
    square = (REPS, REPS)
    starts_r = jnp.sum(
        jnp.where(iota(square, 0) < iota(square, 1), lens_c, 0.0), axis=0, keepdims=True
    )
    starts_c = jnp.sum(
        jnp.where(iota(square, 1) < iota(square, 0), lens_r, 0.0), axis=1, keepdims=True
    )
    shape = (REPS * TPS, REPS)
    mine = place_row[...] == iota(shape, 0) // TPS
    start_g = jnp.sum(jnp.where(mine, starts_r, 0.0), axis=1, keepdims=True).astype(I32)
    shape = (REPS * TPS, TPS * ROUNDS)
    run = lax.rem(iota(shape, 0), TPS)
    round_g = (start_g - (rep * TPS + run) + (DEVICES - 1)) // DEVICES
    col = iota(shape, 1)
    pick[...] = jnp.where(
        (col // ROUNDS == run) & (lax.rem(col, ROUNDS) == round_g), 1.0, 0.0
    ).astype(BF16)
    lanes = 2 * REPS * TPS
    shape = (REPS, lanes)
    mine = place_col[...] == iota(shape, 1) // (2 * TPS)
    start_l = jnp.sum(jnp.where(mine, starts_c, 0.0), axis=0, keepdims=True).astype(I32)
    length_l = jnp.sum(jnp.where(mine, lens_c, 0.0), axis=0, keepdims=True).astype(I32)
    lane = iota((1, lanes), 1)
    order = rep * TPS + lax.rem(lane, TPS)
    round_l = (start_l - order + (DEVICES - 1)) // DEVICES
    live = round_l * DEVICES + order < start_l + length_l
    code = jnp.where(live, round_l + ROUNDS * lax.rem(lane, 2 * TPS), -1)
    shape = (2 * TPS * ROUNDS, lanes)
    place[...] = jnp.where(iota(shape, 0) == code, 1.0, 0.0).astype(BF16)
    own = place_row[...] == rep
    start = jnp.sum(jnp.where(own, starts_r, 0.0), axis=1, keepdims=True).astype(I32)
    length = jnp.sum(jnp.where(own, lens_r, 0.0), axis=1, keepdims=True).astype(I32)
    key_pos = (iota((1, DEVICES), 1) - start) & (DEVICES - 1)
    key_pos = jnp.where(key_pos < length, key_pos, DEVICES)

    pool_copy.wait()
    for i in range(PREFIX // HEAD):
        page = table[0, i]
        keys[pl.ds(i * HEAD, HEAD)] = pool[0, page]
        vals[pl.ds(i * HEAD, HEAD)] = pool[1, page]

    pl.semaphore_wait(barrier, TPS - 1 + REPS - 1)

    def x_parts(head, slot):
        wide = GROUP_HEADS * HEAD
        for source, width, to in (
            (head * wide, wide, 0),
            (QUERY_HEADS * HEAD + head * HEAD, HEAD, wide),
            ((QUERY_HEADS + KEY_VALUE_HEADS) * HEAD + head * HEAD, HEAD, wide + HEAD),
        ):
            yield (
                suffix.at[:, pl.ds(pl.multiple_of(source, HEAD), width)],
                rows_in.at[slot, :, pl.ds(to, width)],
            )

    @pl.loop(1, TPS)
    def _(step):
        to = lax.rem(tp + step, TPS)
        for source, target in x_parts(to, tp):
            pltpu.make_async_remote_copy(
                src_ref=source, dst_ref=target, send_sem=x_send, recv_sem=x_recv,
                device_id=(rep, to), device_id_type=MESH,
            ).start()

    for source, target in x_parts(tp, tp):
        pltpu.make_async_copy(source, target, x_own).start()
    others = rows_in.at[pl.ds(0, TPS - 1)]
    pltpu.make_async_copy(rows_in.at[0], rows_in.at[0], x_own).wait()
    pltpu.make_async_copy(others, others, x_recv).wait()

    def chunk(column):
        tokens = rows_in[:, :, pl.ds(column * HEAD, HEAD)].reshape(TPS * ROUNDS, HEAD)
        return jnp.dot(pick[...], tokens, preferred_element_type=F32).reshape(REPS, TPS, HEAD)

    for part in (KV, *range(PARTS)):
        sent[part] = jnp.concatenate([chunk(2 * part), chunk(2 * part + 1)], axis=1).astype(BF16)

        @pl.loop(1, REPS)
        def _(step):
            to = peer(step)
            pltpu.make_async_remote_copy(
                src_ref=sent.at[part, to], dst_ref=got.at[part, rep],
                send_sem=f_send.at[part], recv_sem=f_recv.at[part],
                device_id=(to, tp), device_id_type=MESH,
            ).start()

        pltpu.make_async_copy(sent.at[part, rep], got.at[part, rep], f_own.at[part]).start()

    def wait_part(ref, recv, local):
        pltpu.make_async_copy(ref.at[0], ref.at[0], local).wait()
        most = ref.at[pl.ds(0, REPS - 1)]
        pltpu.make_async_copy(most, most, recv).wait()

    wait_part(got.at[KV], f_recv.at[KV], f_own.at[KV])
    pair = got[KV].astype(F32)
    keys[pl.ds(PREFIX, DEVICES)] = pair[:, :TPS].reshape(DEVICES, HEAD).astype(BF16)
    vals[pl.ds(PREFIX, DEVICES)] = pair[:, TPS:].reshape(DEVICES, HEAD).astype(BF16)

    factor = math.log2(math.e) / math.sqrt(HEAD)
    tiles = BLOCK // (2 * TPS)
    for part in range(PARTS):
        wait_part(got.at[part], f_recv.at[part], f_own.at[part])

        @pl.loop(0, REPS // tiles)
        def _(step):
            first = pl.multiple_of(step * tiles, tiles)
            query = got[part, pl.ds(first, tiles)].reshape(BLOCK, HEAD)
            row = iota((BLOCK, 1), 0)
            order = (first + row // (2 * TPS)) * TPS + lax.rem(row, TPS)
            pos = (order - start) & (DEVICES - 1)
            scores = lax.dot_general(
                query, keys[...], (((1,), (1,)), ((), ())), preferred_element_type=F32
            )
            before = scores[:, :PREFIX]
            after = jnp.where(key_pos <= pos, scores[:, PREFIX:], -jnp.inf)
            highest = jnp.maximum(
                jnp.max(before, axis=1, keepdims=True), jnp.max(after, axis=1, keepdims=True)
            )
            expo_b = jnp.exp2((before - highest) * factor)
            expo_a = jnp.exp2((after - highest) * factor)
            total = jnp.sum(expo_b, axis=1, keepdims=True) + jnp.sum(expo_a, axis=1, keepdims=True)
            weights = jnp.concatenate([expo_b.astype(BF16), expo_a.astype(BF16)], axis=1)
            mixed = jnp.dot(weights, vals[...], preferred_element_type=F32) / total
            ans[part, pl.ds(first, tiles)] = mixed.astype(BF16).reshape(tiles, 2 * TPS, HEAD)

        @pl.loop(1, REPS)
        def _(step):
            to = peer(step)
            pltpu.make_async_remote_copy(
                src_ref=ans.at[part, to], dst_ref=back.at[part, rep],
                send_sem=b_send.at[part], recv_sem=b_recv.at[part],
                device_id=(to, tp), device_id_type=MESH,
            ).start()

        pltpu.make_async_copy(ans.at[part, rep], back.at[part, rep], b_own.at[part]).start()

    for part in range(PARTS):
        wait_part(back.at[part], b_recv.at[part], b_own.at[part])
        tokens = jnp.dot(
            place[...], back[part].reshape(2 * DEVICES, HEAD), preferred_element_type=F32
        ).astype(BF16).reshape(2, TPS, ROUNDS, HEAD)
        rows_out[part, :, :, pl.ds(0, HEAD)] = tokens[0]
        rows_out[part, :, :, pl.ds(HEAD, HEAD)] = tokens[1]
        column = pl.multiple_of(tp * (GROUP_HEADS * HEAD) + part * 2 * HEAD, HEAD)
        target = out.at[:, pl.ds(column, 2 * HEAD)]

        @pl.loop(1, TPS)
        def _(step):
            to = lax.rem(tp + step, TPS)
            pltpu.make_async_remote_copy(
                src_ref=rows_out.at[part, to], dst_ref=target,
                send_sem=o_send, recv_sem=o_recv,
                device_id=(rep, to), device_id_type=MESH,
            ).start()

        pltpu.make_async_copy(rows_out.at[part, tp], target, o_own).start()

    pltpu.make_async_copy(others, others, x_send).wait()
    for part in range(PARTS + 1):
        most = sent.at[part, pl.ds(0, REPS - 1)]
        pltpu.make_async_copy(most, most, f_send.at[part]).wait()
    for part in range(PARTS):
        most = ans.at[part, pl.ds(0, REPS - 1)]
        pltpu.make_async_copy(most, most, b_send.at[part]).wait()
    most = rows_out.at[:, pl.ds(0, TPS - 1)]
    pltpu.make_async_copy(most, most, o_send).wait()
    pltpu.make_async_copy(most, most, o_recv).wait()
    mine = rows_out.at[:, 0]
    pltpu.make_async_copy(mine, mine, o_own).wait()


def shards(suffix, key_value_pages, placement, lengths, page_table):
    message = (PARTS, REPS, 2 * TPS, HEAD)
    dma = pltpu.SemaphoreType.DMA
    anywhere = pl.BlockSpec(memory_space=pl.ANY)
    vmem = pl.BlockSpec(memory_space=pltpu.VMEM)
    width = (GROUP_HEADS + 2) * HEAD
    return pl.pallas_call(
        kernel,
        out_shape=jax.ShapeDtypeStruct((ROUNDS, QUERY_HEADS * HEAD), BF16),
        in_specs=[anywhere] * 2 + [vmem] * 4 + [pl.BlockSpec(memory_space=pltpu.SMEM)],
        out_specs=anywhere,
        scratch_shapes=[
            pltpu.VMEM((TPS, ROUNDS, width), BF16),
            pltpu.VMEM(key_value_pages.shape, BF16),
            pltpu.VMEM((REPS * TPS, TPS * ROUNDS), BF16),
            pltpu.VMEM((2 * TPS * ROUNDS, 2 * REPS * TPS), BF16),
            pltpu.VMEM((PREFIX + DEVICES, HEAD), BF16),
            pltpu.VMEM((PREFIX + DEVICES, HEAD), BF16),
            pltpu.VMEM((PARTS + 1, *message[1:]), BF16),
            pltpu.VMEM((PARTS + 1, *message[1:]), BF16),
            pltpu.VMEM(message, BF16),
            pltpu.VMEM(message, BF16),
            pltpu.VMEM((PARTS, TPS, ROUNDS, 2 * HEAD), BF16),
            dma, dma, dma, dma,
            dma((PARTS + 1,)), dma((PARTS + 1,)), dma((PARTS + 1,)),
            dma((PARTS,)), dma((PARTS,)), dma((PARTS,)),
            dma, dma, dma,
        ],
        compiler_params=pltpu.CompilerParams(
            collective_id=0, has_side_effects=True, vmem_limit_bytes=40 * 2**20
        ),
        cost_estimate=pl.CostEstimate(
            flops=4 * 4096 * 1024 * HEAD, bytes_accessed=2**20, transcendentals=4096 * 1024
        ),
    )(
        suffix,
        key_value_pages,
        placement.reshape(1, REPS),
        placement.reshape(REPS, 1),
        lengths.reshape(1, REPS),
        lengths.reshape(REPS, 1),
        page_table,
    )


def solution(mesh):
    return jax.shard_map(
        shards,
        mesh=mesh,
        in_specs=(P(("rep", "tp"), None), P(None, "rep", None, "tp"), P(), P(), P("rep", None)),
        out_specs=P(("rep", "tp"), None),
        check_vma=False,
    )
```

```python
import functools
import math

import jax
import jax.numpy as jnp
from jax import lax
from jax.experimental import pallas as pl
from jax.experimental.pallas import tpu as pltpu
from jax.sharding import PartitionSpec as P

QUERY_HEADS = 64
KEY_VALUE_HEADS = 8
HEAD = 128
REPS = 64
TPS = 8
ROUNDS = 16
DEVICES = REPS * TPS
GROUP_HEADS = QUERY_HEADS // TPS
PARTS = GROUP_HEADS // 2
KV = PARTS
PREFIX = 512
BLOCK = 128
MESH = pl.DeviceIdType.MESH
F32 = jnp.float32
I32 = jnp.int32
BF16 = jnp.bfloat16


def iota(shape, dim):
    return lax.broadcasted_iota(I32, shape, dim)


def one_hot(code, width):
    return jnp.where(iota((code.shape[0], width), 1) == code, 1.0, 0.0).astype(BF16)


def kernel(
    suffix, pages, placement, lengths, page_table, out,
    place_row, len_row, table, rows, heads_in, pool, pick, place, keys, vals, sent, got, pairs_out,
    ans_out, ans_in, ans, back, rows_back,
    small_sem, rows_sem, pool_sem, x_send, x_recv, x_own, k_send, k_recv, k_own, f_send, f_recv, f_own,
    a_send, a_recv, a_own, b_send, b_recv, b_own, out_sem,
):
    rep = lax.axis_index("rep")
    tp = lax.axis_index("tp")
    z, y = rep >> 3, rep & 7

    def peer(step):
        a, b = step >> 3, step & 7
        return (((z + a + b) & 7) << 3) + ((y + b) & 7)

    rows_copy = pltpu.make_async_copy(suffix, rows, rows_sem)
    rows_copy.start()
    small = [
        pltpu.make_async_copy(source, target, small_sem.at[i])
        for i, (source, target) in enumerate(
            ((placement, place_row), (lengths, len_row), (page_table, table))
        )
    ]
    for copy in small:
        copy.start()
    pool_copy = pltpu.make_async_copy(pages, pool, pool_sem)
    pool_copy.start()

    barrier = pltpu.get_barrier_semaphore()

    @pl.loop(1, REPS)
    def _(step):
        pl.semaphore_signal(barrier, inc=1, device_id=(peer(step), tp), device_id_type=MESH)

    @pl.loop(1, TPS)
    def _(step):
        pl.semaphore_signal(
            barrier, inc=1, device_id=(rep, (tp + step) & (TPS - 1)), device_id_type=MESH
        )

    def along_tp(copies, send, recv, own):
        @pl.loop(1, TPS)
        def _(step):
            to = (tp + step) & (TPS - 1)
            for source, target in copies(to):
                pltpu.make_async_remote_copy(
                    src_ref=source, dst_ref=target, send_sem=send, recv_sem=recv,
                    device_id=(rep, to), device_id_type=MESH,
                ).start()

        for source, target in copies(tp):
            pltpu.make_async_copy(source, target, own).start()

    def over_plane(source, target, send, recv, own):
        @pl.loop(1, REPS)
        def _(step):
            to = peer(step)
            pltpu.make_async_remote_copy(
                src_ref=source.at[to], dst_ref=target.at[rep], send_sem=send, recv_sem=recv,
                device_id=(to, tp), device_id_type=MESH,
            ).start()

        pltpu.make_async_copy(source.at[rep], target.at[rep], own).start()

    def wait_bytes(ref, count, sem):
        some = ref.at[pl.ds(0, count)]
        pltpu.make_async_copy(some, some, sem).wait()

    for copy in small:
        copy.wait()
    square = (REPS, REPS)
    lens_r = len_row[...].astype(F32)
    diagonal = iota(square, 0) == iota(square, 1)
    lens_c = jnp.sum(jnp.where(diagonal, lens_r, 0.0), axis=1, keepdims=True)
    starts_r = jnp.sum(
        jnp.where(iota(square, 0) < iota(square, 1), lens_c, 0.0), axis=0, keepdims=True
    )
    place_r = place_row[...]

    def round_of(start, order):
        return (start - order + (DEVICES - 1)) >> 9

    count = REPS * 2 * TPS
    row = iota((count, 1), 0)
    mine = place_r == iota((count, REPS), 0) >> 4
    start_g = jnp.sum(jnp.where(mine, starts_r, 0.0), axis=1, keepdims=True).astype(I32)
    round_g = round_of(start_g, rep * TPS + tp)
    code = jnp.where(round_g < ROUNDS, round_g + (row & (2 * TPS - 1)) * ROUNDS, -1)
    rows_copy.wait()
    pairs = jnp.concatenate(
        [rows[:, pl.ds((QUERY_HEADS + i) * HEAD, HEAD)] for i in range(2 * KEY_VALUE_HEADS)], axis=0
    )
    sent[KV] = (
        jnp.dot(one_hot(code, 2 * TPS * ROUNDS), pairs, preferred_element_type=F32)
        .astype(BF16)
        .reshape(REPS, 2 * TPS, HEAD)
    )

    pl.semaphore_wait(barrier, TPS - 1 + REPS - 1)

    def queries_along_tp(part):
        def copies(to):
            first = pl.multiple_of(to * (GROUP_HEADS * HEAD) + part * 2 * HEAD, HEAD)
            return ((rows.at[:, pl.ds(first, 2 * HEAD)], heads_in.at[part, tp]),)

        along_tp(copies, x_send.at[part], x_recv.at[part], x_own.at[part])

    queries_along_tp(0)
    over_plane(sent.at[KV], got.at[KV], f_send.at[KV], f_recv.at[KV], f_own.at[KV])
    for part in range(1, PARTS):
        queries_along_tp(part)

    run = iota((REPS * TPS, 1), 0) & (TPS - 1)
    mine = place_r == iota((REPS * TPS, REPS), 0) >> 3
    start_g = jnp.sum(jnp.where(mine, starts_r, 0.0), axis=1, keepdims=True).astype(I32)
    round_g = round_of(start_g, rep * TPS + run)
    pick[...] = one_hot(
        jnp.where(round_g < ROUNDS, round_g + run * ROUNDS, -1), TPS * ROUNDS
    )

    def chunk(part, half):
        tokens = heads_in[part, :, :, pl.ds(half * HEAD, HEAD)].reshape(TPS * ROUNDS, HEAD)
        return jnp.dot(pick[...], tokens, preferred_element_type=F32).reshape(REPS, TPS, HEAD)

    for part in range(PARTS):
        wait_bytes(heads_in.at[part], 1, x_own.at[part])
        wait_bytes(heads_in.at[part], TPS - 1, x_recv.at[part])
        sent[part] = jnp.concatenate([chunk(part, 0), chunk(part, 1)], axis=1).astype(BF16)
        over_plane(sent.at[part], got.at[part], f_send.at[part], f_recv.at[part], f_own.at[part])

    def wait_part(ref, recv, own):
        wait_bytes(ref, 1, own)
        wait_bytes(ref, REPS - 1, recv)

    turn = iota((256, 1), 0)
    turn = one_hot(((turn & 15) << 4) + (turn >> 4), 256)
    wait_part(got.at[KV], f_recv.at[KV], f_own.at[KV])
    for i in range(REPS // 16):
        block = got[KV, pl.ds(i * 16, 16)].reshape(256, HEAD)
        pairs_out[:, pl.ds(i * 16, 16)] = (
            jnp.dot(turn, block, preferred_element_type=F32).astype(BF16).reshape(16, 16, HEAD)
        )
    to_here = pl.ds(pl.multiple_of(PREFIX + tp * REPS, REPS), REPS)
    along_tp(
        lambda to: (
            (pairs_out.at[to], keys.at[to_here]),
            (pairs_out.at[TPS + to], vals.at[to_here]),
        ),
        k_send, k_recv, k_own,
    )

    place_c = jnp.sum(
        jnp.where(diagonal, place_r.astype(F32), 0.0), axis=1, keepdims=True
    ).astype(I32)
    starts_c = jnp.sum(
        jnp.where(iota(square, 1) < iota(square, 0), lens_r, 0.0), axis=1, keepdims=True
    )
    mine = place_c == iota((REPS, count), 1) >> 4
    start_l = jnp.sum(jnp.where(mine, starts_c, 0.0), axis=0, keepdims=True).astype(I32)
    length_l = jnp.sum(jnp.where(mine, lens_c, 0.0), axis=0, keepdims=True).astype(I32)
    order = rep * TPS + tp
    round_l = round_of(start_l, order)
    live = round_l * DEVICES + order < start_l + length_l
    code = round_l + ROUNDS * (iota((1, count), 1) & (2 * TPS - 1))
    shape = (2 * TPS * ROUNDS, count)
    place[...] = jnp.where(iota(shape, 0) == jnp.where(live, code, -1), 1.0, 0.0).astype(BF16)
    own = place_r == rep
    start = jnp.sum(jnp.where(own, starts_r, 0.0), axis=1, keepdims=True).astype(I32)
    length = jnp.sum(jnp.where(own, lens_r, 0.0), axis=1, keepdims=True).astype(I32)
    lane = iota((1, DEVICES), 1)
    key_pos = ((lane & (REPS - 1)) * TPS + (lane >> 6) - start) & (DEVICES - 1)
    key_pos = jnp.where(key_pos < length, key_pos, DEVICES)

    pool_copy.wait()
    for i in range(PREFIX // HEAD):
        page = table[0, i]
        keys[pl.ds(i * HEAD, HEAD)] = pool[0, page]
        vals[pl.ds(i * HEAD, HEAD)] = pool[1, page]

    wait_bytes(pairs_out, 2, k_own)
    wait_bytes(pairs_out, 2 * (TPS - 1), k_recv)

    factor = math.log2(math.e) / math.sqrt(HEAD)
    tiles = BLOCK // (2 * TPS)
    index = iota((BLOCK, 1), 0)
    by_place = one_hot((((index >> 1) & 7) << 4) + ((index & 1) << 3) + (index >> 4), BLOCK)
    by_rep = one_hot((((index >> 1) & 7) << 4) + ((index >> 4) << 1) + (index & 1), BLOCK)

    def attend(part):
        wait_part(got.at[part], f_recv.at[part], f_own.at[part])

        @pl.loop(0, REPS // tiles)
        def _(step):
            first = pl.multiple_of(step * tiles, tiles)
            query = got[part, pl.ds(first, tiles)].reshape(BLOCK, HEAD)
            order = (first + (index >> 4)) * TPS + (index & (TPS - 1))
            pos = (order - start) & (DEVICES - 1)
            scores = lax.dot_general(
                query, keys[...], (((1,), (1,)), ((), ())), preferred_element_type=F32
            )
            before = scores[:, :PREFIX]
            after = jnp.where(key_pos <= pos, scores[:, PREFIX:], -jnp.inf)
            highest = jnp.maximum(
                jnp.max(before, axis=1, keepdims=True), jnp.max(after, axis=1, keepdims=True)
            )
            expo_b = jnp.exp2((before - highest) * factor)
            expo_a = jnp.exp2((after - highest) * factor)
            total = jnp.sum(expo_b, axis=1, keepdims=True) + jnp.sum(expo_a, axis=1, keepdims=True)
            weights = jnp.concatenate([expo_b.astype(BF16), expo_a.astype(BF16)], axis=1)
            mixed = jnp.dot(weights, vals[...], preferred_element_type=F32) / total
            mixed = jnp.dot(by_place, mixed.astype(BF16), preferred_element_type=F32).astype(BF16)
            to = pl.multiple_of(step * 2 * tiles, 2 * tiles)
            ans_out[part, :, pl.ds(to, 2 * tiles)] = mixed.reshape(TPS, 2 * tiles, HEAD)

        along_tp(
            lambda to: ((ans_out.at[part, to], ans_in.at[part, tp]),),
            a_send.at[part], a_recv.at[part], a_own.at[part],
        )

    def answer(part):
        wait_bytes(ans_in.at[part], 1, a_own.at[part])
        wait_bytes(ans_in.at[part], TPS - 1, a_recv.at[part])
        for i in range(REPS // tiles):
            block = ans_in[part, :, pl.ds(i * 2 * tiles, 2 * tiles)].reshape(BLOCK, HEAD)
            ans[part, pl.ds(i * tiles, tiles)] = (
                jnp.dot(by_rep, block, preferred_element_type=F32)
                .astype(BF16)
                .reshape(tiles, 2 * TPS, HEAD)
            )
        over_plane(ans.at[part], back.at[part], b_send.at[part], b_recv.at[part], b_own.at[part])

    for part in range(PARTS):
        attend(part)
        if part > 0:
            answer(part - 1)
    answer(PARTS - 1)

    for part in range(PARTS):
        wait_part(back.at[part], b_recv.at[part], b_own.at[part])
        tokens = jnp.dot(
            place[...], back[part].reshape(count, HEAD), preferred_element_type=F32
        ).astype(BF16).reshape(TPS, 2, ROUNDS, HEAD)
        for head in range(TPS):
            for half in range(2):
                column = (head * GROUP_HEADS + 2 * part + half) * HEAD
                rows_back[:, pl.ds(column, HEAD)] = tokens[head, half]
    out_copy = pltpu.make_async_copy(rows_back, out, out_sem)
    out_copy.start()
    for part in range(PARTS):
        wait_bytes(heads_in.at[part], TPS - 1, x_send.at[part])
        wait_bytes(ans_out.at[part], TPS - 1, a_send.at[part])
        wait_bytes(ans.at[part], REPS - 1, b_send.at[part])
    for part in range(PARTS + 1):
        wait_bytes(sent.at[part], REPS - 1, f_send.at[part])
    wait_bytes(pairs_out, 2 * (TPS - 1), k_send)
    out_copy.wait()


def shards(suffix, key_value_pages, placement, lengths, page_table):
    message = (REPS, 2 * TPS, HEAD)
    dma = pltpu.SemaphoreType.DMA
    parts = dma((PARTS,))
    anywhere = pl.BlockSpec(memory_space=pltpu.HBM)
    return pl.pallas_call(
        kernel,
        out_shape=jax.ShapeDtypeStruct((ROUNDS, QUERY_HEADS * HEAD), BF16),
        in_specs=[anywhere] * 5,
        out_specs=anywhere,
        scratch_shapes=[
            pltpu.VMEM((1, REPS), I32),
            pltpu.VMEM((1, REPS), I32),
            pltpu.SMEM(page_table.shape, I32),
            pltpu.VMEM(suffix.shape, BF16),
            pltpu.VMEM((PARTS, TPS, ROUNDS, 2 * HEAD), BF16),
            pltpu.VMEM(key_value_pages.shape, BF16),
            pltpu.VMEM((REPS * TPS, TPS * ROUNDS), BF16),
            pltpu.VMEM((2 * TPS * ROUNDS, 2 * REPS * TPS), BF16),
            pltpu.VMEM((PREFIX + DEVICES, HEAD), BF16),
            pltpu.VMEM((PREFIX + DEVICES, HEAD), BF16),
            pltpu.VMEM((PARTS + 1, *message), BF16),
            pltpu.VMEM((PARTS + 1, *message), BF16),
            pltpu.VMEM((2 * TPS, REPS, HEAD), BF16),
            pltpu.VMEM((PARTS, TPS, 2 * REPS, HEAD), BF16),
            pltpu.VMEM((PARTS, TPS, 2 * REPS, HEAD), BF16),
            pltpu.VMEM((PARTS, *message), BF16),
            pltpu.VMEM((PARTS, *message), BF16),
            pltpu.VMEM((ROUNDS, QUERY_HEADS * HEAD), BF16),
            dma((3,)), dma, dma,
            parts, parts, parts,
            dma, dma, dma,
            dma((PARTS + 1,)), dma((PARTS + 1,)), dma((PARTS + 1,)),
            parts, parts, parts,
            parts, parts, parts,
            dma,
        ],
        compiler_params=pltpu.CompilerParams(
            collective_id=0, has_side_effects=True, vmem_limit_bytes=60 * 2**20
        ),
        cost_estimate=pl.CostEstimate(
            flops=4 * 4096 * 1024 * HEAD, bytes_accessed=2**20, transcendentals=4096 * 1024
        ),
    )(
        suffix,
        key_value_pages,
        placement.reshape(1, REPS),
        lengths.reshape(1, REPS),
        page_table,
    )


def solution(mesh):
    return jax.shard_map(
        shards,
        mesh=mesh,
        in_specs=(P(("rep", "tp"), None), P(None, "rep", None, "tp"), P(), P(), P("rep", None)),
        out_specs=P(("rep", "tp"), None),
        check_vma=False,
    )
```

```python
import functools
import math

import jax
import jax.numpy as jnp
from jax import lax
from jax.experimental import pallas as pl
from jax.experimental.pallas import tpu as pltpu
from jax.sharding import PartitionSpec as P

QUERY_HEADS = 64
KEY_VALUE_HEADS = 8
HEAD = 128
REPS = 64
TPS = 8
ROUNDS = 16
DEVICES = REPS * TPS
GROUP_HEADS = QUERY_HEADS // TPS
PARTS = GROUP_HEADS // 2
KV = PARTS
PREFIX = 512
BLOCK = 128
LONGEST = 384
RUNS = LONGEST // TPS + 1
MESH = pl.DeviceIdType.MESH
F32 = jnp.float32
I32 = jnp.int32
BF16 = jnp.bfloat16


def iota(shape, dim):
    return lax.broadcasted_iota(I32, shape, dim)


def one_hot(code, width):
    return jnp.where(iota((code.shape[0], width), 1) == code, 1.0, 0.0).astype(BF16)


def kernel(
    suffix, pages, placement, lengths, page_table, out,
    place_row, len_row, place_s, len_s, table, rows, heads_in, pool, pick, place, keys_in, vals_in, keys, vals, sent, got_0, got_1, got_2, got_3, got_kv, pairs_out, queries, mixed,
    ans_out, ans_in, ans, back, rows_back,
    small_sem, rows_sem, pool_sem, x_send, x_recv, x_own, k_send, k_recv, k_own, f_send, f_recv, f_own,
    a_send, a_recv, a_own, b_send, b_recv, b_own, out_sem,
):
    got = (got_0, got_1, got_2, got_3, got_kv)
    rep = lax.axis_index("rep")
    tp = lax.axis_index("tp")
    z, y = rep >> 3, rep & 7

    def peer(step):
        a, b = step >> 3, step & 7
        return (((z + a + b) & 7) << 3) + ((y + b) & 7)

    rows_copy = pltpu.make_async_copy(suffix, rows, rows_sem)
    rows_copy.start()
    small = [
        pltpu.make_async_copy(source, target, small_sem.at[i])
        for i, (source, target) in enumerate(
            (
                (placement, place_row), (lengths, len_row),
                (placement, place_s), (lengths, len_s), (page_table, table),
            )
        )
    ]
    for copy in small:
        copy.start()
    pool_copy = pltpu.make_async_copy(pages, pool, pool_sem)
    pool_copy.start()

    barrier = pltpu.get_barrier_semaphore()

    @pl.loop(1, REPS)
    def _(step):
        pl.semaphore_signal(barrier, inc=1, device_id=(peer(step), tp), device_id_type=MESH)

    @pl.loop(1, TPS)
    def _(step):
        pl.semaphore_signal(
            barrier, inc=1, device_id=(rep, (tp + step) & (TPS - 1)), device_id_type=MESH
        )

    def along_tp(copies, send, recv, own):
        @pl.loop(1, TPS)
        def _(step):
            to = (tp + step) & (TPS - 1)
            for source, target in copies(to):
                pltpu.make_async_remote_copy(
                    src_ref=source, dst_ref=target, send_sem=send, recv_sem=recv,
                    device_id=(rep, to), device_id_type=MESH,
                ).start()

        for source, target in copies(tp):
            pltpu.make_async_copy(source, target, own).start()

    def over_plane(source, target, send, recv, own):
        @pl.loop(1, REPS)
        def _(step):
            to = peer(step)
            pltpu.make_async_remote_copy(
                src_ref=source.at[to], dst_ref=target.at[rep], send_sem=send, recv_sem=recv,
                device_id=(to, tp), device_id_type=MESH,
            ).start()

        pltpu.make_async_copy(source.at[rep], target.at[rep], own).start()

    def wait_bytes(ref, count, sem):
        some = ref.at[pl.ds(0, count)]
        pltpu.make_async_copy(some, some, sem).wait()

    for copy in small:
        copy.wait()
    square = (REPS, REPS)
    lens_r = len_row[...].astype(F32)
    diagonal = iota(square, 0) == iota(square, 1)
    lens_c = jnp.sum(jnp.where(diagonal, lens_r, 0.0), axis=1, keepdims=True)
    starts_r = jnp.sum(
        jnp.where(iota(square, 0) < iota(square, 1), lens_c, 0.0), axis=0, keepdims=True
    )
    place_r = place_row[...]

    def round_of(start, order):
        return (start - order + (DEVICES - 1)) >> 9

    count = REPS * 2 * TPS
    row = iota((count, 1), 0)
    mine = place_r == iota((count, REPS), 0) >> 4
    start_g = jnp.sum(jnp.where(mine, starts_r, 0.0), axis=1, keepdims=True).astype(I32)
    round_g = round_of(start_g, rep * TPS + tp)
    code = jnp.where(round_g < ROUNDS, round_g + (row & (2 * TPS - 1)) * ROUNDS, -1)
    rows_copy.wait()
    pairs = jnp.concatenate(
        [rows[:, pl.ds((QUERY_HEADS + i) * HEAD, HEAD)] for i in range(2 * KEY_VALUE_HEADS)], axis=0
    )
    sent[KV] = (
        jnp.dot(one_hot(code, 2 * TPS * ROUNDS), pairs, preferred_element_type=F32)
        .astype(BF16)
        .reshape(REPS, 2 * TPS, HEAD)
    )

    pl.semaphore_wait(barrier, TPS - 1 + REPS - 1)

    def queries_along_tp(part):
        def copies(to):
            first = pl.multiple_of(to * (GROUP_HEADS * HEAD) + part * 2 * HEAD, HEAD)
            return ((rows.at[:, pl.ds(first, 2 * HEAD)], heads_in.at[part, tp]),)

        along_tp(copies, x_send.at[part], x_recv.at[part], x_own.at[part])

    queries_along_tp(0)
    over_plane(sent.at[KV], got[KV], f_send.at[KV], f_recv.at[KV], f_own.at[KV])
    for part in range(1, PARTS):
        queries_along_tp(part)

    run = iota((REPS * TPS, 1), 0) & (TPS - 1)
    mine = place_r == iota((REPS * TPS, REPS), 0) >> 3
    start_g = jnp.sum(jnp.where(mine, starts_r, 0.0), axis=1, keepdims=True).astype(I32)
    round_g = round_of(start_g, rep * TPS + run)
    pick[...] = one_hot(
        jnp.where(round_g < ROUNDS, round_g + run * ROUNDS, -1), TPS * ROUNDS
    )

    def chunk(part, half):
        tokens = heads_in[part, :, :, pl.ds(half * HEAD, HEAD)].reshape(TPS * ROUNDS, HEAD)
        return jnp.dot(pick[...], tokens, preferred_element_type=F32).reshape(REPS, TPS, HEAD)

    for part in range(PARTS):
        wait_bytes(heads_in.at[part], 1, x_own.at[part])
        wait_bytes(heads_in.at[part], TPS - 1, x_recv.at[part])
        sent[part] = jnp.concatenate([chunk(part, 0), chunk(part, 1)], axis=1).astype(BF16)
        over_plane(sent.at[part], got[part], f_send.at[part], f_recv.at[part], f_own.at[part])

    def wait_part(ref, recv, own):
        wait_bytes(ref, 1, own)
        wait_bytes(ref, REPS - 1, recv)

    turn = iota((256, 1), 0)
    turn = one_hot(((turn & 15) << 4) + (turn >> 4), 256)
    wait_part(got[KV], f_recv.at[KV], f_own.at[KV])
    for i in range(REPS // 16):
        block = got[KV][pl.ds(i * 16, 16)].reshape(256, HEAD)
        pairs_out[:, pl.ds(i * 16, 16)] = (
            jnp.dot(turn, block, preferred_element_type=F32).astype(BF16).reshape(16, 16, HEAD)
        )
    to_here = pl.ds(pl.multiple_of(tp * REPS, REPS), REPS)
    along_tp(
        lambda to: (
            (pairs_out.at[to], keys_in.at[to_here]),
            (pairs_out.at[TPS + to], vals_in.at[to_here]),
        ),
        k_send, k_recv, k_own,
    )

    place_c = jnp.sum(
        jnp.where(diagonal, place_r.astype(F32), 0.0), axis=1, keepdims=True
    ).astype(I32)
    starts_c = jnp.sum(
        jnp.where(iota(square, 1) < iota(square, 0), lens_r, 0.0), axis=1, keepdims=True
    )
    mine = place_c == iota((REPS, count), 1) >> 4
    start_l = jnp.sum(jnp.where(mine, starts_c, 0.0), axis=0, keepdims=True).astype(I32)
    length_l = jnp.sum(jnp.where(mine, lens_c, 0.0), axis=0, keepdims=True).astype(I32)
    order = rep * TPS + tp
    round_l = round_of(start_l, order)
    live = round_l * DEVICES + order < start_l + length_l
    code = round_l + ROUNDS * (iota((1, count), 1) & (2 * TPS - 1))
    shape = (2 * TPS * ROUNDS, count)
    place[...] = jnp.where(iota(shape, 0) == jnp.where(live, code, -1), 1.0, 0.0).astype(BF16)
    def add(r, carry):
        before, start = carry
        return before + len_s[0, r], start + jnp.where(place_s[0, r] == rep, before, 0)

    start = lax.fori_loop(0, REPS, add, (jnp.int32(0), jnp.int32(0)))[1]
    length = jnp.sum(jnp.where(place_r == rep, lens_r, 0.0), axis=1, keepdims=True).astype(I32)
    first_rep, shift = (start >> 3) & (REPS - 1), start & (TPS - 1)

    factor = math.log2(math.e) / math.sqrt(HEAD)

    def store_keys(first, block):
        scaled = block.astype(F32) * factor
        high = scaled.astype(BF16)
        keys[pl.ds(first, block.shape[0]), pl.ds(0, HEAD)] = high
        keys[pl.ds(first, block.shape[0]), pl.ds(HEAD, HEAD)] = (
            scaled - high.astype(F32)
        ).astype(BF16)

    pool_copy.wait()
    for i in range(PREFIX // HEAD):
        page = table[0, i]
        store_keys(i * HEAD, pool[0, page])
        vals[pl.ds(i * HEAD, HEAD)] = pool[1, page]
    mixed[...] = jnp.zeros_like(mixed)

    lane = iota((1, DEVICES), 1)
    pos = ((lane & (REPS - 1)) * TPS + (lane >> 6) - start) & (DEVICES - 1)
    pos = jnp.where(pos < length, pos, DEVICES)
    in_order = jnp.where(iota((LONGEST, DEVICES), 0) == pos, 1.0, 0.0).astype(BF16)
    wait_bytes(pairs_out, 2, k_own)
    wait_bytes(pairs_out, 2 * (TPS - 1), k_recv)
    store_keys(PREFIX, jnp.dot(in_order, keys_in[...], preferred_element_type=F32))
    vals[pl.ds(PREFIX, LONGEST)] = jnp.dot(
        in_order, vals_in[...], preferred_element_type=F32
    ).astype(BF16)

    tiles = BLOCK // (2 * TPS)
    index = iota((BLOCK, 1), 0)
    by_place = one_hot((((index >> 1) & 7) << 4) + ((index & 1) << 3) + (index >> 4), BLOCK)
    by_rep = one_hot((((index >> 1) & 7) << 4) + ((index >> 4) << 1) + (index & 1), BLOCK)

    def attend_runs(first, count, reach):
        height = count * 2 * TPS
        query = queries[pl.ds(first, count)].reshape(height, HEAD)
        row = iota((height, 1), 0)
        pos = (first + (row >> 4)) * TPS + (row & (TPS - 1)) - shift
        width = PREFIX + reach
        scores = lax.dot_general(
            jnp.concatenate([query, query], axis=1), keys[pl.ds(0, width)],
            (((1,), (1,)), ((), ())), preferred_element_type=F32,
        )
        seen = PREFIX + max(0, (first * TPS - TPS) // HEAD * HEAD)
        column = iota((1, width - seen), 1) + (seen - PREFIX)
        after = jnp.where(column <= pos, scores[:, seen:], -jnp.inf)
        scores = jnp.concatenate([scores[:, :seen], after], axis=1)
        expo = jnp.exp2(scores - jnp.max(scores, axis=1, keepdims=True))
        total = jnp.sum(expo, axis=1, keepdims=True)
        result = jnp.dot(expo.astype(BF16), vals[pl.ds(0, width)], preferred_element_type=F32)
        mixed[pl.ds(first, count)] = (result / total).astype(BF16).reshape(count, 2 * TPS, HEAD)

    def arrive(part):
        wait_part(got[part], f_recv.at[part], f_own.at[part])

    def attend(part):
        for run in range(RUNS):
            queries[run] = got[part][(first_rep + run) & (REPS - 1)]
        step = HEAD // TPS
        for i in range(LONGEST // HEAD):
            last = i == LONGEST // HEAD - 1
            attend_runs(i * step, step + (RUNS - LONGEST // TPS if last else 0), (i + 1) * HEAD)
        for i in range(REPS // tiles):
            block = [mixed[(i * tiles + m - first_rep) & (REPS - 1)] for m in range(tiles)]
            block = jnp.dot(by_place, jnp.concatenate(block, axis=0), preferred_element_type=F32)
            ans_out[part, :, pl.ds(i * 2 * tiles, 2 * tiles)] = block.astype(BF16).reshape(
                TPS, 2 * tiles, HEAD
            )
        along_tp(
            lambda to: ((ans_out.at[part, to], ans_in.at[part, tp]),),
            a_send.at[part], a_recv.at[part], a_own.at[part],
        )

    def prepare(part):
        wait_bytes(ans_in.at[part], 1, a_own.at[part])
        wait_bytes(ans_in.at[part], TPS - 1, a_recv.at[part])
        for i in range(REPS // tiles):
            block = ans_in[part, :, pl.ds(i * 2 * tiles, 2 * tiles)].reshape(BLOCK, HEAD)
            ans[part, pl.ds(i * tiles, tiles)] = (
                jnp.dot(by_rep, block, preferred_element_type=F32)
                .astype(BF16)
                .reshape(tiles, 2 * TPS, HEAD)
            )

    def answer(part):
        over_plane(ans.at[part], back.at[part], b_send.at[part], b_recv.at[part], b_own.at[part])

    arrive(0)
    attend(0)
    arrive(1)
    attend(1)
    prepare(0)
    answer(0)
    arrive(2)
    attend(2)
    prepare(1)
    answer(1)
    arrive(3)
    attend(3)
    prepare(2)
    answer(2)
    prepare(3)
    answer(3)

    for part in range(PARTS):
        wait_part(back.at[part], b_recv.at[part], b_own.at[part])
        tokens = jnp.dot(
            place[...], back[part].reshape(count, HEAD), preferred_element_type=F32
        ).astype(BF16).reshape(TPS, 2, ROUNDS, HEAD)
        for head in range(TPS):
            for half in range(2):
                column = (head * GROUP_HEADS + 2 * part + half) * HEAD
                rows_back[:, pl.ds(column, HEAD)] = tokens[head, half]
    out_copy = pltpu.make_async_copy(rows_back, out, out_sem)
    out_copy.start()
    for part in range(PARTS):
        wait_bytes(heads_in.at[part], TPS - 1, x_send.at[part])
        wait_bytes(ans_out.at[part], TPS - 1, a_send.at[part])
        wait_bytes(ans.at[part], REPS - 1, b_send.at[part])
    for part in range(PARTS + 1):
        wait_bytes(sent.at[part], REPS - 1, f_send.at[part])
    wait_bytes(pairs_out, 2 * (TPS - 1), k_send)
    out_copy.wait()


def shards(suffix, key_value_pages, placement, lengths, page_table):
    message = (REPS, 2 * TPS, HEAD)
    dma = pltpu.SemaphoreType.DMA
    parts = dma((PARTS,))
    anywhere = pl.BlockSpec(memory_space=pltpu.HBM)
    return pl.pallas_call(
        kernel,
        out_shape=jax.ShapeDtypeStruct((ROUNDS, QUERY_HEADS * HEAD), BF16),
        in_specs=[anywhere] * 5,
        out_specs=anywhere,
        scratch_shapes=[
            pltpu.VMEM((1, REPS), I32),
            pltpu.VMEM((1, REPS), I32),
            pltpu.SMEM((1, REPS), I32),
            pltpu.SMEM((1, REPS), I32),
            pltpu.SMEM(page_table.shape, I32),
            pltpu.VMEM(suffix.shape, BF16),
            pltpu.VMEM((PARTS, TPS, ROUNDS, 2 * HEAD), BF16),
            pltpu.VMEM(key_value_pages.shape, BF16),
            pltpu.VMEM((REPS * TPS, TPS * ROUNDS), BF16),
            pltpu.VMEM((2 * TPS * ROUNDS, 2 * REPS * TPS), BF16),
            pltpu.VMEM((DEVICES, HEAD), BF16),
            pltpu.VMEM((DEVICES, HEAD), BF16),
            pltpu.VMEM((PREFIX + LONGEST, 2 * HEAD), BF16),
            pltpu.VMEM((PREFIX + LONGEST, HEAD), BF16),
            pltpu.VMEM((PARTS + 1, *message), BF16),
            *[pltpu.VMEM(message, BF16)] * (PARTS + 1),
            pltpu.VMEM((2 * TPS, REPS, HEAD), BF16),
            pltpu.VMEM((RUNS, 2 * TPS, HEAD), BF16),
            pltpu.VMEM(message, BF16),
            pltpu.VMEM((PARTS, TPS, 2 * REPS, HEAD), BF16),
            pltpu.VMEM((PARTS, TPS, 2 * REPS, HEAD), BF16),
            pltpu.VMEM((PARTS, *message), BF16),
            pltpu.VMEM((PARTS, *message), BF16),
            pltpu.VMEM((ROUNDS, QUERY_HEADS * HEAD), BF16),
            dma((5,)), dma, dma,
            parts, parts, parts,
            dma, dma, dma,
            dma((PARTS + 1,)), dma((PARTS + 1,)), dma((PARTS + 1,)),
            parts, parts, parts,
            parts, parts, parts,
            dma,
        ],
        compiler_params=pltpu.CompilerParams(
            collective_id=0, has_side_effects=True, vmem_limit_bytes=60 * 2**20
        ),
        cost_estimate=pl.CostEstimate(
            flops=4 * 4096 * 1024 * HEAD, bytes_accessed=2**20, transcendentals=4096 * 1024
        ),
    )(
        suffix,
        key_value_pages,
        placement.reshape(1, REPS),
        lengths.reshape(1, REPS),
        page_table,
    )


def solution(mesh):
    return jax.shard_map(
        shards,
        mesh=mesh,
        in_specs=(P(("rep", "tp"), None), P(None, "rep", None, "tp"), P(), P(), P("rep", None)),
        out_specs=P(("rep", "tp"), None),
        check_vma=False,
    )
```

```python
import functools
import math

import jax
import jax.numpy as jnp
from jax import lax
from jax.experimental import pallas as pl
from jax.experimental.pallas import tpu as pltpu
from jax.sharding import PartitionSpec as P

QUERY_HEADS = 64
KEY_VALUE_HEADS = 8
HEAD = 128
REPS = 64
TPS = 8
ROUNDS = 16
DEVICES = REPS * TPS
GROUP_HEADS = QUERY_HEADS // TPS
PARTS = GROUP_HEADS // 2
KV = PARTS
PREFIX = 512
BLOCK = 128
LONGEST = 384
RUNS = LONGEST // TPS + 1
MESH = pl.DeviceIdType.MESH
F32 = jnp.float32
I32 = jnp.int32
BF16 = jnp.bfloat16


def iota(shape, dim):
    return lax.broadcasted_iota(I32, shape, dim)


def one_hot(code, width):
    return jnp.where(iota((code.shape[0], width), 1) == code, 1.0, 0.0).astype(BF16)


def kernel(
    suffix, pages, placement, lengths, page_table, out,
    place_row, len_row, place_s, len_s, table, rows, heads_in, pool, pick, place, keys_in, vals_in, keys, vals, sent, got_0, got_1, got_2, got_3, got_kv, pairs_out, queries, mixed,
    ans_out, ans_in, ans, back, rows_back,
    small_sem, rows_sem, pool_sem, x_send, x_recv, x_own, k_send, k_recv, k_own, f_send, f_recv, f_own,
    a_send, a_recv, a_own, b_send, b_recv, b_own, out_sem,
):
    got = (got_0, got_1, got_2, got_3, got_kv)
    rep = lax.axis_index("rep")
    tp = lax.axis_index("tp")
    z, y = rep >> 3, rep & 7

    def peer(step):
        a, b = step >> 3, step & 7
        return (((z + b) & 7) << 3) + ((y + a + b) & 7)

    rows_copy = pltpu.make_async_copy(suffix, rows, rows_sem)
    rows_copy.start()
    small = [
        pltpu.make_async_copy(source, target, small_sem.at[i])
        for i, (source, target) in enumerate(
            (
                (placement, place_row), (lengths, len_row),
                (placement, place_s), (lengths, len_s), (page_table, table),
            )
        )
    ]
    for copy in small:
        copy.start()
    pool_copy = pltpu.make_async_copy(pages, pool, pool_sem)
    pool_copy.start()

    barrier = pltpu.get_barrier_semaphore()

    @pl.loop(1, REPS)
    def _(step):
        pl.semaphore_signal(barrier, inc=1, device_id=(peer(step), tp), device_id_type=MESH)

    @pl.loop(1, TPS)
    def _(step):
        pl.semaphore_signal(
            barrier, inc=1, device_id=(rep, (tp + step) & (TPS - 1)), device_id_type=MESH
        )

    def along_tp(copies, send, recv, own):
        @pl.loop(1, TPS)
        def _(step):
            to = (tp + step) & (TPS - 1)
            for source, target in copies(to):
                pltpu.make_async_remote_copy(
                    src_ref=source, dst_ref=target, send_sem=send, recv_sem=recv,
                    device_id=(rep, to), device_id_type=MESH,
                ).start()

        for source, target in copies(tp):
            pltpu.make_async_copy(source, target, own).start()

    def over_plane(source, target, send, recv, own):
        @pl.loop(1, REPS)
        def _(step):
            to = peer(step)
            pltpu.make_async_remote_copy(
                src_ref=source.at[to], dst_ref=target.at[rep], send_sem=send, recv_sem=recv,
                device_id=(to, tp), device_id_type=MESH,
            ).start()

        pltpu.make_async_copy(source.at[rep], target.at[rep], own).start()

    def wait_bytes(ref, count, sem):
        some = ref.at[pl.ds(0, count)]
        pltpu.make_async_copy(some, some, sem).wait()

    for copy in small:
        copy.wait()
    square = (REPS, REPS)
    lens_r = len_row[...].astype(F32)
    diagonal = iota(square, 0) == iota(square, 1)
    lens_c = jnp.sum(jnp.where(diagonal, lens_r, 0.0), axis=1, keepdims=True)
    starts_r = jnp.sum(
        jnp.where(iota(square, 0) < iota(square, 1), lens_c, 0.0), axis=0, keepdims=True
    )
    place_r = place_row[...]

    def round_of(start, order):
        return (start - order + (DEVICES - 1)) >> 9

    count = REPS * 2 * TPS
    row = iota((count, 1), 0)
    mine = place_r == iota((count, REPS), 0) >> 4
    start_g = jnp.sum(jnp.where(mine, starts_r, 0.0), axis=1, keepdims=True).astype(I32)
    round_g = round_of(start_g, rep * TPS + tp)
    code = jnp.where(round_g < ROUNDS, round_g + (row & (2 * TPS - 1)) * ROUNDS, -1)
    rows_copy.wait()
    pairs = jnp.concatenate(
        [rows[:, pl.ds((QUERY_HEADS + i) * HEAD, HEAD)] for i in range(2 * KEY_VALUE_HEADS)], axis=0
    )
    sent[KV] = (
        jnp.dot(one_hot(code, 2 * TPS * ROUNDS), pairs, preferred_element_type=F32)
        .astype(BF16)
        .reshape(REPS, 2 * TPS, HEAD)
    )

    pl.semaphore_wait(barrier, TPS - 1 + REPS - 1)

    def queries_along_tp(part):
        def copies(to):
            first = pl.multiple_of(to * (GROUP_HEADS * HEAD) + part * 2 * HEAD, HEAD)
            return ((rows.at[:, pl.ds(first, 2 * HEAD)], heads_in.at[part, tp]),)

        along_tp(copies, x_send.at[part], x_recv.at[part], x_own.at[part])

    queries_along_tp(0)
    over_plane(sent.at[KV], got[KV], f_send.at[KV], f_recv.at[KV], f_own.at[KV])
    for part in range(1, PARTS):
        queries_along_tp(part)

    run = iota((REPS * TPS, 1), 0) & (TPS - 1)
    mine = place_r == iota((REPS * TPS, REPS), 0) >> 3
    start_g = jnp.sum(jnp.where(mine, starts_r, 0.0), axis=1, keepdims=True).astype(I32)
    round_g = round_of(start_g, rep * TPS + run)
    pick[...] = one_hot(
        jnp.where(round_g < ROUNDS, round_g + run * ROUNDS, -1), TPS * ROUNDS
    )

    def chunk(part, half):
        tokens = heads_in[part, :, :, pl.ds(half * HEAD, HEAD)].reshape(TPS * ROUNDS, HEAD)
        return jnp.dot(pick[...], tokens, preferred_element_type=F32).reshape(REPS, TPS, HEAD)

    for part in range(PARTS):
        wait_bytes(heads_in.at[part], 1, x_own.at[part])
        wait_bytes(heads_in.at[part], TPS - 1, x_recv.at[part])
        sent[part] = jnp.concatenate([chunk(part, 0), chunk(part, 1)], axis=1).astype(BF16)
        over_plane(sent.at[part], got[part], f_send.at[part], f_recv.at[part], f_own.at[part])

    def wait_part(ref, recv, own):
        wait_bytes(ref, 1, own)
        wait_bytes(ref, REPS - 1, recv)

    turn = iota((256, 1), 0)
    turn = one_hot(((turn & 15) << 4) + (turn >> 4), 256)
    wait_part(got[KV], f_recv.at[KV], f_own.at[KV])
    for i in range(REPS // 16):
        block = got[KV][pl.ds(i * 16, 16)].reshape(256, HEAD)
        pairs_out[:, pl.ds(i * 16, 16)] = (
            jnp.dot(turn, block, preferred_element_type=F32).astype(BF16).reshape(16, 16, HEAD)
        )
    to_here = pl.ds(pl.multiple_of(tp * REPS, REPS), REPS)
    along_tp(
        lambda to: (
            (pairs_out.at[to], keys_in.at[to_here]),
            (pairs_out.at[TPS + to], vals_in.at[to_here]),
        ),
        k_send, k_recv, k_own,
    )

    place_c = jnp.sum(
        jnp.where(diagonal, place_r.astype(F32), 0.0), axis=1, keepdims=True
    ).astype(I32)
    starts_c = jnp.sum(
        jnp.where(iota(square, 1) < iota(square, 0), lens_r, 0.0), axis=1, keepdims=True
    )
    mine = place_c == iota((REPS, count), 1) >> 4
    start_l = jnp.sum(jnp.where(mine, starts_c, 0.0), axis=0, keepdims=True).astype(I32)
    length_l = jnp.sum(jnp.where(mine, lens_c, 0.0), axis=0, keepdims=True).astype(I32)
    order = rep * TPS + tp
    round_l = round_of(start_l, order)
    live = round_l * DEVICES + order < start_l + length_l
    code = round_l + ROUNDS * (iota((1, count), 1) & (2 * TPS - 1))
    shape = (2 * TPS * ROUNDS, count)
    place[...] = jnp.where(iota(shape, 0) == jnp.where(live, code, -1), 1.0, 0.0).astype(BF16)
    def add(r, carry):
        before, start = carry
        return before + len_s[0, r], start + jnp.where(place_s[0, r] == rep, before, 0)

    start = lax.fori_loop(0, REPS, add, (jnp.int32(0), jnp.int32(0)))[1]
    length = jnp.sum(jnp.where(place_r == rep, lens_r, 0.0), axis=1, keepdims=True).astype(I32)
    first_rep, shift = (start >> 3) & (REPS - 1), start & (TPS - 1)

    factor = math.log2(math.e) / math.sqrt(HEAD)

    def store_keys(first, block):
        scaled = block.astype(F32) * factor
        high = scaled.astype(BF16)
        keys[pl.ds(first, block.shape[0]), pl.ds(0, HEAD)] = high
        keys[pl.ds(first, block.shape[0]), pl.ds(HEAD, HEAD)] = (
            scaled - high.astype(F32)
        ).astype(BF16)

    pool_copy.wait()
    for i in range(PREFIX // HEAD):
        page = table[0, i]
        store_keys(i * HEAD, pool[0, page])
        vals[pl.ds(i * HEAD, HEAD)] = pool[1, page]
    mixed[...] = jnp.zeros_like(mixed)

    lane = iota((1, DEVICES), 1)
    pos = ((lane & (REPS - 1)) * TPS + (lane >> 6) - start) & (DEVICES - 1)
    pos = jnp.where(pos < length, pos, DEVICES)
    in_order = jnp.where(iota((LONGEST, DEVICES), 0) == pos, 1.0, 0.0).astype(BF16)
    wait_bytes(pairs_out, 2, k_own)
    wait_bytes(pairs_out, 2 * (TPS - 1), k_recv)
    store_keys(PREFIX, jnp.dot(in_order, keys_in[...], preferred_element_type=F32))
    vals[pl.ds(PREFIX, LONGEST)] = jnp.dot(
        in_order, vals_in[...], preferred_element_type=F32
    ).astype(BF16)

    tiles = BLOCK // (2 * TPS)
    index = iota((BLOCK, 1), 0)
    by_place = one_hot((((index >> 1) & 7) << 4) + ((index & 1) << 3) + (index >> 4), BLOCK)
    by_rep = one_hot((((index >> 1) & 7) << 4) + ((index >> 4) << 1) + (index & 1), BLOCK)

    def attend_runs(first, count, reach):
        height = count * 2 * TPS
        query = queries[pl.ds(first, count)].reshape(height, HEAD)
        row = iota((height, 1), 0)
        pos = (first + (row >> 4)) * TPS + (row & (TPS - 1)) - shift
        width = PREFIX + reach
        scores = lax.dot_general(
            jnp.concatenate([query, query], axis=1), keys[pl.ds(0, width)],
            (((1,), (1,)), ((), ())), preferred_element_type=F32,
        )
        seen = PREFIX + max(0, (first * TPS - TPS) // HEAD * HEAD)
        column = iota((1, width - seen), 1) + (seen - PREFIX)
        after = jnp.where(column <= pos, scores[:, seen:], -jnp.inf)
        scores = jnp.concatenate([scores[:, :seen], after], axis=1)
        expo = jnp.exp2(scores - jnp.max(scores, axis=1, keepdims=True))
        total = jnp.sum(expo, axis=1, keepdims=True)
        result = jnp.dot(expo.astype(BF16), vals[pl.ds(0, width)], preferred_element_type=F32)
        mixed[pl.ds(first, count)] = (result / total).astype(BF16).reshape(count, 2 * TPS, HEAD)

    def arrive(part):
        wait_part(got[part], f_recv.at[part], f_own.at[part])

    def attend(part):
        for run in range(RUNS):
            queries[run] = got[part][(first_rep + run) & (REPS - 1)]
        step = HEAD // TPS
        for i in range(LONGEST // HEAD):
            last = i == LONGEST // HEAD - 1
            attend_runs(i * step, step + (RUNS - LONGEST // TPS if last else 0), (i + 1) * HEAD)
        for i in range(REPS // tiles):
            block = [mixed[(i * tiles + m - first_rep) & (REPS - 1)] for m in range(tiles)]
            block = jnp.dot(by_place, jnp.concatenate(block, axis=0), preferred_element_type=F32)
            ans_out[part, :, pl.ds(i * 2 * tiles, 2 * tiles)] = block.astype(BF16).reshape(
                TPS, 2 * tiles, HEAD
            )
        along_tp(
            lambda to: ((ans_out.at[part, to], ans_in.at[part, tp]),),
            a_send.at[part], a_recv.at[part], a_own.at[part],
        )

    def prepare(part):
        wait_bytes(ans_in.at[part], 1, a_own.at[part])
        wait_bytes(ans_in.at[part], TPS - 1, a_recv.at[part])
        for i in range(REPS // tiles):
            block = ans_in[part, :, pl.ds(i * 2 * tiles, 2 * tiles)].reshape(BLOCK, HEAD)
            ans[part, pl.ds(i * tiles, tiles)] = (
                jnp.dot(by_rep, block, preferred_element_type=F32)
                .astype(BF16)
                .reshape(tiles, 2 * TPS, HEAD)
            )

    def answer(part):
        over_plane(ans.at[part], back.at[part], b_send.at[part], b_recv.at[part], b_own.at[part])

    arrive(0)
    attend(0)
    arrive(1)
    attend(1)
    prepare(0)
    answer(0)
    arrive(2)
    attend(2)
    prepare(1)
    answer(1)
    arrive(3)
    attend(3)
    prepare(2)
    answer(2)
    prepare(3)
    answer(3)

    for part in range(PARTS):
        wait_part(back.at[part], b_recv.at[part], b_own.at[part])
        tokens = jnp.dot(
            place[...], back[part].reshape(count, HEAD), preferred_element_type=F32
        ).astype(BF16).reshape(TPS, 2, ROUNDS, HEAD)
        for head in range(TPS):
            for half in range(2):
                column = (head * GROUP_HEADS + 2 * part + half) * HEAD
                rows_back[:, pl.ds(column, HEAD)] = tokens[head, half]
    out_copy = pltpu.make_async_copy(rows_back, out, out_sem)
    out_copy.start()
    for part in range(PARTS):
        wait_bytes(heads_in.at[part], TPS - 1, x_send.at[part])
        wait_bytes(ans_out.at[part], TPS - 1, a_send.at[part])
        wait_bytes(ans.at[part], REPS - 1, b_send.at[part])
    for part in range(PARTS + 1):
        wait_bytes(sent.at[part], REPS - 1, f_send.at[part])
    wait_bytes(pairs_out, 2 * (TPS - 1), k_send)
    out_copy.wait()


def shards(suffix, key_value_pages, placement, lengths, page_table):
    message = (REPS, 2 * TPS, HEAD)
    dma = pltpu.SemaphoreType.DMA
    parts = dma((PARTS,))
    anywhere = pl.BlockSpec(memory_space=pl.ANY)
    return pl.pallas_call(
        kernel,
        out_shape=jax.ShapeDtypeStruct((ROUNDS, QUERY_HEADS * HEAD), BF16),
        in_specs=[anywhere] * 5,
        out_specs=anywhere,
        scratch_shapes=[
            pltpu.VMEM((1, REPS), I32),
            pltpu.VMEM((1, REPS), I32),
            pltpu.SMEM((1, REPS), I32),
            pltpu.SMEM((1, REPS), I32),
            pltpu.SMEM(page_table.shape, I32),
            pltpu.VMEM(suffix.shape, BF16),
            pltpu.VMEM((PARTS, TPS, ROUNDS, 2 * HEAD), BF16),
            pltpu.VMEM(key_value_pages.shape, BF16),
            pltpu.VMEM((REPS * TPS, TPS * ROUNDS), BF16),
            pltpu.VMEM((2 * TPS * ROUNDS, 2 * REPS * TPS), BF16),
            pltpu.VMEM((DEVICES, HEAD), BF16),
            pltpu.VMEM((DEVICES, HEAD), BF16),
            pltpu.VMEM((PREFIX + LONGEST, 2 * HEAD), BF16),
            pltpu.VMEM((PREFIX + LONGEST, HEAD), BF16),
            pltpu.VMEM((PARTS + 1, *message), BF16),
            *[pltpu.VMEM(message, BF16)] * (PARTS + 1),
            pltpu.VMEM((2 * TPS, REPS, HEAD), BF16),
            pltpu.VMEM((RUNS, 2 * TPS, HEAD), BF16),
            pltpu.VMEM(message, BF16),
            pltpu.VMEM((PARTS, TPS, 2 * REPS, HEAD), BF16),
            pltpu.VMEM((PARTS, TPS, 2 * REPS, HEAD), BF16),
            pltpu.VMEM((PARTS, *message), BF16),
            pltpu.VMEM((PARTS, *message), BF16),
            pltpu.VMEM((ROUNDS, QUERY_HEADS * HEAD), BF16),
            dma((5,)), dma, dma,
            parts, parts, parts,
            dma, dma, dma,
            dma((PARTS + 1,)), dma((PARTS + 1,)), dma((PARTS + 1,)),
            parts, parts, parts,
            parts, parts, parts,
            dma,
        ],
        compiler_params=pltpu.CompilerParams(
            collective_id=0, has_side_effects=True, vmem_limit_bytes=56_100_000
        ),
        cost_estimate=pl.CostEstimate(
            flops=4 * 4096 * 1024 * HEAD, bytes_accessed=2**20, transcendentals=4096 * 1024
        ),
    )(
        suffix,
        key_value_pages,
        placement.reshape(1, REPS),
        lengths.reshape(1, REPS),
        page_table,
    )


def solution(mesh):
    return jax.shard_map(
        shards,
        mesh=mesh,
        in_specs=(P(("rep", "tp"), None), P(None, "rep", None, "tp"), P(), P(), P("rep", None)),
        out_specs=P(("rep", "tp"), None),
        check_vma=False,
    )
```

```python
import functools
import math

import jax
import jax.numpy as jnp
from jax import lax
from jax.experimental import pallas as pl
from jax.experimental.pallas import tpu as pltpu
from jax.sharding import PartitionSpec as P

QUERY_HEADS = 64
KEY_VALUE_HEADS = 8
HEAD = 128
REPS = 64
TPS = 8
ROUNDS = 16
DEVICES = REPS * TPS
GROUP_HEADS = QUERY_HEADS // TPS
PARTS = GROUP_HEADS // 2
KV = PARTS
PREFIX = 512
BLOCK = 128
LONGEST = 384
RUNS = LONGEST // TPS + 1
MESH = pl.DeviceIdType.MESH
F32 = jnp.float32
I32 = jnp.int32
BF16 = jnp.bfloat16


def iota(shape, dim):
    return lax.broadcasted_iota(I32, shape, dim)


def one_hot(code, width):
    return jnp.where(iota((code.shape[0], width), 1) == code, 1.0, 0.0).astype(BF16)


def kernel(
    suffix, pages, placement, lengths, page_table, out,
    place_row, len_row, place_s, len_s, table, rows, heads_in, pool, pick, place, keys_in, vals_in, keys, vals, sent, got_0, got_1, got_2, got_3, got_kv, pairs_out, queries, mixed,
    ans_out, ans_in, ans, back,
    small_sem, rows_sem, pool_sem, x_send, x_recv, x_own, k_send, k_recv, k_own, f_send, f_recv, f_own,
    a_send, a_recv, a_own, b_send, b_recv, b_own,
):
    got = (got_0, got_1, got_2, got_3, got_kv)
    rep = lax.axis_index("rep")
    tp = lax.axis_index("tp")
    z, y = rep >> 3, rep & 7

    def peer(step):
        a, b = step >> 3, step & 7
        return (((z + b) & 7) << 3) + ((y + a + 3 * b) & 7)

    rows_copy = pltpu.make_async_copy(suffix, rows, rows_sem)
    rows_copy.start()
    small = [
        pltpu.make_async_copy(source, target, small_sem.at[i])
        for i, (source, target) in enumerate(
            (
                (placement, place_row), (lengths, len_row),
                (placement, place_s), (lengths, len_s), (page_table, table),
            )
        )
    ]
    for copy in small:
        copy.start()
    pool_copy = pltpu.make_async_copy(pages, pool, pool_sem)
    pool_copy.start()

    barrier = pltpu.get_barrier_semaphore()

    @pl.loop(1, REPS)
    def _(step):
        pl.semaphore_signal(barrier, inc=1, device_id=(peer(step), tp), device_id_type=MESH)

    @pl.loop(1, TPS)
    def _(step):
        pl.semaphore_signal(
            barrier, inc=1, device_id=(rep, (tp + step) & (TPS - 1)), device_id_type=MESH
        )

    def along_tp(copies, send, recv, own):
        @pl.loop(1, TPS)
        def _(step):
            to = (tp + step) & (TPS - 1)
            for source, target in copies(to):
                pltpu.make_async_remote_copy(
                    src_ref=source, dst_ref=target, send_sem=send, recv_sem=recv,
                    device_id=(rep, to), device_id_type=MESH,
                ).start()

        for source, target in copies(tp):
            pltpu.make_async_copy(source, target, own).start()

    def over_plane(source, target, send, recv, own):
        @pl.loop(1, REPS)
        def _(step):
            to = peer(step)
            pltpu.make_async_remote_copy(
                src_ref=source.at[to], dst_ref=target.at[rep], send_sem=send, recv_sem=recv,
                device_id=(to, tp), device_id_type=MESH,
            ).start()

        pltpu.make_async_copy(source.at[rep], target.at[rep], own).start()

    def wait_bytes(ref, count, sem):
        some = ref.at[pl.ds(0, count)]
        pltpu.make_async_copy(some, some, sem).wait()

    for copy in small:
        copy.wait()
    square = (REPS, REPS)
    lens_r = len_row[...].astype(F32)
    diagonal = iota(square, 0) == iota(square, 1)
    lens_c = jnp.sum(jnp.where(diagonal, lens_r, 0.0), axis=1, keepdims=True)
    starts_r = jnp.sum(
        jnp.where(iota(square, 0) < iota(square, 1), lens_c, 0.0), axis=0, keepdims=True
    )
    place_r = place_row[...]

    def round_of(start, order):
        return (start - order + (DEVICES - 1)) >> 9

    count = REPS * 2 * TPS
    row = iota((count, 1), 0)
    mine = place_r == iota((count, REPS), 0) >> 4
    start_g = jnp.sum(jnp.where(mine, starts_r, 0.0), axis=1, keepdims=True).astype(I32)
    round_g = round_of(start_g, rep * TPS + tp)
    code = jnp.where(round_g < ROUNDS, round_g + (row & (2 * TPS - 1)) * ROUNDS, -1)
    rows_copy.wait()
    pairs = jnp.concatenate(
        [rows[:, pl.ds((QUERY_HEADS + i) * HEAD, HEAD)] for i in range(2 * KEY_VALUE_HEADS)], axis=0
    )
    sent[KV] = (
        jnp.dot(one_hot(code, 2 * TPS * ROUNDS), pairs, preferred_element_type=F32)
        .astype(BF16)
        .reshape(REPS, 2 * TPS, HEAD)
    )

    pl.semaphore_wait(barrier, TPS - 1 + REPS - 1)

    def queries_along_tp(part):
        def copies(to):
            first = pl.multiple_of(to * (GROUP_HEADS * HEAD) + part * 2 * HEAD, HEAD)
            return ((rows.at[:, pl.ds(first, 2 * HEAD)], heads_in.at[part, tp]),)

        along_tp(copies, x_send.at[part], x_recv.at[part], x_own.at[part])

    queries_along_tp(0)
    over_plane(sent.at[KV], got[KV], f_send.at[KV], f_recv.at[KV], f_own.at[KV])
    for part in range(1, PARTS):
        queries_along_tp(part)

    run = iota((REPS * TPS, 1), 0) & (TPS - 1)
    mine = place_r == iota((REPS * TPS, REPS), 0) >> 3
    start_g = jnp.sum(jnp.where(mine, starts_r, 0.0), axis=1, keepdims=True).astype(I32)
    round_g = round_of(start_g, rep * TPS + run)
    pick[...] = one_hot(
        jnp.where(round_g < ROUNDS, round_g + run * ROUNDS, -1), TPS * ROUNDS
    )

    def chunk(part, half):
        tokens = heads_in[part, :, :, pl.ds(half * HEAD, HEAD)].reshape(TPS * ROUNDS, HEAD)
        return jnp.dot(pick[...], tokens, preferred_element_type=F32).reshape(REPS, TPS, HEAD)

    for part in range(PARTS):
        wait_bytes(heads_in.at[part], 1, x_own.at[part])
        wait_bytes(heads_in.at[part], TPS - 1, x_recv.at[part])
        sent[part] = jnp.concatenate([chunk(part, 0), chunk(part, 1)], axis=1).astype(BF16)
        over_plane(sent.at[part], got[part], f_send.at[part], f_recv.at[part], f_own.at[part])

    def wait_part(ref, recv, own):
        wait_bytes(ref, 1, own)
        wait_bytes(ref, REPS - 1, recv)

    turn = iota((256, 1), 0)
    turn = one_hot(((turn & 15) << 4) + (turn >> 4), 256)
    wait_part(got[KV], f_recv.at[KV], f_own.at[KV])
    for i in range(REPS // 16):
        block = got[KV][pl.ds(i * 16, 16)].reshape(256, HEAD)
        pairs_out[:, pl.ds(i * 16, 16)] = (
            jnp.dot(turn, block, preferred_element_type=F32).astype(BF16).reshape(16, 16, HEAD)
        )
    to_here = pl.ds(pl.multiple_of(tp * REPS, REPS), REPS)
    along_tp(
        lambda to: (
            (pairs_out.at[to], keys_in.at[to_here]),
            (pairs_out.at[TPS + to], vals_in.at[to_here]),
        ),
        k_send, k_recv, k_own,
    )

    place_c = jnp.sum(
        jnp.where(diagonal, place_r.astype(F32), 0.0), axis=1, keepdims=True
    ).astype(I32)
    starts_c = jnp.sum(
        jnp.where(iota(square, 1) < iota(square, 0), lens_r, 0.0), axis=1, keepdims=True
    )
    mine = place_c == iota((REPS, count), 1) >> 4
    start_l = jnp.sum(jnp.where(mine, starts_c, 0.0), axis=0, keepdims=True).astype(I32)
    length_l = jnp.sum(jnp.where(mine, lens_c, 0.0), axis=0, keepdims=True).astype(I32)
    order = rep * TPS + tp
    round_l = round_of(start_l, order)
    live = round_l * DEVICES + order < start_l + length_l
    code = round_l + ROUNDS * (iota((1, count), 1) & (2 * TPS - 1))
    shape = (2 * TPS * ROUNDS, count)
    place[...] = jnp.where(iota(shape, 0) == jnp.where(live, code, -1), 1.0, 0.0).astype(BF16)
    def add(r, carry):
        before, start = carry
        return before + len_s[0, r], start + jnp.where(place_s[0, r] == rep, before, 0)

    start = lax.fori_loop(0, REPS, add, (jnp.int32(0), jnp.int32(0)))[1]
    length = jnp.sum(jnp.where(place_r == rep, lens_r, 0.0), axis=1, keepdims=True).astype(I32)
    first_rep, shift = (start >> 3) & (REPS - 1), start & (TPS - 1)

    factor = math.log2(math.e) / math.sqrt(HEAD)

    def store_keys(first, block):
        scaled = block.astype(F32) * factor
        high = scaled.astype(BF16)
        keys[pl.ds(first, block.shape[0]), pl.ds(0, HEAD)] = high
        keys[pl.ds(first, block.shape[0]), pl.ds(HEAD, HEAD)] = (
            scaled - high.astype(F32)
        ).astype(BF16)

    pool_copy.wait()
    for i in range(PREFIX // HEAD):
        page = table[0, i]
        store_keys(i * HEAD, pool[0, page])
        vals[pl.ds(i * HEAD, HEAD)] = pool[1, page]
    mixed[...] = jnp.zeros_like(mixed)

    lane = iota((1, DEVICES), 1)
    pos = ((lane & (REPS - 1)) * TPS + (lane >> 6) - start) & (DEVICES - 1)
    pos = jnp.where(pos < length, pos, DEVICES)
    in_order = jnp.where(iota((LONGEST, DEVICES), 0) == pos, 1.0, 0.0).astype(BF16)
    wait_bytes(pairs_out, 2, k_own)
    wait_bytes(pairs_out, 2 * (TPS - 1), k_recv)
    store_keys(PREFIX, jnp.dot(in_order, keys_in[...], preferred_element_type=F32))
    vals[pl.ds(PREFIX, LONGEST)] = jnp.dot(
        in_order, vals_in[...], preferred_element_type=F32
    ).astype(BF16)

    tiles = BLOCK // (2 * TPS)
    index = iota((BLOCK, 1), 0)
    by_place = one_hot((((index >> 1) & 7) << 4) + ((index & 1) << 3) + (index >> 4), BLOCK)
    by_rep = one_hot((((index >> 1) & 7) << 4) + ((index >> 4) << 1) + (index & 1), BLOCK)

    def attend_runs(first, count, reach):
        height = count * 2 * TPS
        query = queries[pl.ds(first, count)].reshape(height, HEAD)
        row = iota((height, 1), 0)
        pos = (first + (row >> 4)) * TPS + (row & (TPS - 1)) - shift
        width = PREFIX + reach
        scores = lax.dot_general(
            jnp.concatenate([query, query], axis=1), keys[pl.ds(0, width)],
            (((1,), (1,)), ((), ())), preferred_element_type=F32,
        )
        seen = PREFIX + max(0, (first * TPS - TPS) // HEAD * HEAD)
        column = iota((1, width - seen), 1) + (seen - PREFIX)
        after = jnp.where(column <= pos, scores[:, seen:], -jnp.inf)
        scores = jnp.concatenate([scores[:, :seen], after], axis=1)
        expo = jnp.exp2(scores - jnp.max(scores, axis=1, keepdims=True))
        total = jnp.sum(expo, axis=1, keepdims=True)
        result = jnp.dot(expo.astype(BF16), vals[pl.ds(0, width)], preferred_element_type=F32)
        mixed[pl.ds(first, count)] = (result / total).astype(BF16).reshape(count, 2 * TPS, HEAD)

    def arrive(part):
        wait_part(got[part], f_recv.at[part], f_own.at[part])

    def attend(part):
        for run in range(RUNS):
            queries[run] = got[part][(first_rep + run) & (REPS - 1)]
        step = HEAD // TPS
        for i in range(LONGEST // HEAD):
            last = i == LONGEST // HEAD - 1
            attend_runs(i * step, step + (RUNS - LONGEST // TPS if last else 0), (i + 1) * HEAD)
        for i in range(REPS // tiles):
            block = [mixed[(i * tiles + m - first_rep) & (REPS - 1)] for m in range(tiles)]
            block = jnp.dot(by_place, jnp.concatenate(block, axis=0), preferred_element_type=F32)
            ans_out[part, :, pl.ds(i * 2 * tiles, 2 * tiles)] = block.astype(BF16).reshape(
                TPS, 2 * tiles, HEAD
            )
        along_tp(
            lambda to: ((ans_out.at[part, to], ans_in.at[part, tp]),),
            a_send.at[part], a_recv.at[part], a_own.at[part],
        )

    def prepare(part):
        wait_bytes(ans_in.at[part], 1, a_own.at[part])
        wait_bytes(ans_in.at[part], TPS - 1, a_recv.at[part])
        for i in range(REPS // tiles):
            block = ans_in[part, :, pl.ds(i * 2 * tiles, 2 * tiles)].reshape(BLOCK, HEAD)
            ans[part, pl.ds(i * tiles, tiles)] = (
                jnp.dot(by_rep, block, preferred_element_type=F32)
                .astype(BF16)
                .reshape(tiles, 2 * TPS, HEAD)
            )

    def answer(part):
        over_plane(ans.at[part], back.at[part], b_send.at[part], b_recv.at[part], b_own.at[part])

    arrive(0)
    attend(0)
    arrive(1)
    attend(1)
    prepare(0)
    answer(0)
    arrive(2)
    attend(2)
    prepare(1)
    answer(1)
    arrive(3)
    attend(3)
    prepare(2)
    answer(2)
    prepare(3)
    answer(3)

    for part in range(PARTS):
        wait_part(back.at[part], b_recv.at[part], b_own.at[part])
        tokens = jnp.dot(
            place[...], back[part].reshape(count, HEAD), preferred_element_type=F32
        ).astype(BF16).reshape(TPS, 2, ROUNDS, HEAD)
        for head in range(TPS):
            for half in range(2):
                column = (head * GROUP_HEADS + 2 * part + half) * HEAD
                out[:, pl.ds(column, HEAD)] = tokens[head, half]
    for part in range(PARTS):
        wait_bytes(heads_in.at[part], TPS - 1, x_send.at[part])
        wait_bytes(ans_out.at[part], TPS - 1, a_send.at[part])
        wait_bytes(ans.at[part], REPS - 1, b_send.at[part])
    for part in range(PARTS + 1):
        wait_bytes(sent.at[part], REPS - 1, f_send.at[part])
    wait_bytes(pairs_out, 2 * (TPS - 1), k_send)


def shards(suffix, key_value_pages, placement, lengths, page_table):
    message = (REPS, 2 * TPS, HEAD)
    dma = pltpu.SemaphoreType.DMA
    parts = dma((PARTS,))
    anywhere = pl.BlockSpec(memory_space=pl.ANY)
    return pl.pallas_call(
        kernel,
        out_shape=jax.ShapeDtypeStruct((ROUNDS, QUERY_HEADS * HEAD), BF16),
        in_specs=[anywhere] * 5,
        out_specs=pl.BlockSpec(memory_space=pltpu.VMEM),
        scratch_shapes=[
            pltpu.VMEM((1, REPS), I32),
            pltpu.VMEM((1, REPS), I32),
            pltpu.SMEM((1, REPS), I32),
            pltpu.SMEM((1, REPS), I32),
            pltpu.SMEM(page_table.shape, I32),
            pltpu.VMEM(suffix.shape, BF16),
            pltpu.VMEM((PARTS, TPS, ROUNDS, 2 * HEAD), BF16),
            pltpu.VMEM(key_value_pages.shape, BF16),
            pltpu.VMEM((REPS * TPS, TPS * ROUNDS), BF16),
            pltpu.VMEM((2 * TPS * ROUNDS, 2 * REPS * TPS), BF16),
            pltpu.VMEM((DEVICES, HEAD), BF16),
            pltpu.VMEM((DEVICES, HEAD), BF16),
            pltpu.VMEM((PREFIX + LONGEST, 2 * HEAD), BF16),
            pltpu.VMEM((PREFIX + LONGEST, HEAD), BF16),
            pltpu.VMEM((PARTS + 1, *message), BF16),
            *[pltpu.VMEM(message, BF16)] * (PARTS + 1),
            pltpu.VMEM((2 * TPS, REPS, HEAD), BF16),
            pltpu.VMEM((RUNS, 2 * TPS, HEAD), BF16),
            pltpu.VMEM(message, BF16),
            pltpu.VMEM((PARTS, TPS, 2 * REPS, HEAD), BF16),
            pltpu.VMEM((PARTS, TPS, 2 * REPS, HEAD), BF16),
            pltpu.VMEM((PARTS, *message), BF16),
            pltpu.VMEM((PARTS, *message), BF16),
            dma((5,)), dma, dma,
            parts, parts, parts,
            dma, dma, dma,
            dma((PARTS + 1,)), dma((PARTS + 1,)), dma((PARTS + 1,)),
            parts, parts, parts,
            parts, parts, parts,
        ],
        compiler_params=pltpu.CompilerParams(
            collective_id=0, has_side_effects=True, vmem_limit_bytes=56_100_000
        ),
        cost_estimate=pl.CostEstimate(
            flops=4 * 4096 * 1024 * HEAD, bytes_accessed=2**20, transcendentals=4096 * 1024
        ),
    )(
        suffix,
        key_value_pages,
        placement.reshape(1, REPS),
        lengths.reshape(1, REPS),
        page_table,
    )


def solution(mesh):
    return jax.shard_map(
        shards,
        mesh=mesh,
        in_specs=(P(("rep", "tp"), None), P(None, "rep", None, "tp"), P(), P(), P("rep", None)),
        out_specs=P(("rep", "tp"), None),
        check_vma=False,
    )
```

```python
import functools
import math

import jax
import jax.numpy as jnp
from jax import lax
from jax.experimental import pallas as pl
from jax.experimental.pallas import tpu as pltpu
from jax.sharding import PartitionSpec as P

QUERY_HEADS = 64
KEY_VALUE_HEADS = 8
HEAD = 128
REPS = 64
TPS = 8
ROUNDS = 16
DEVICES = REPS * TPS
GROUP_HEADS = QUERY_HEADS // TPS
PARTS = GROUP_HEADS // 2
KV = PARTS
PREFIX = 512
BLOCK = 128
LONGEST = 384
RUNS = LONGEST // TPS + 1
MESH = pl.DeviceIdType.MESH
F32 = jnp.float32
I32 = jnp.int32
BF16 = jnp.bfloat16


def iota(shape, dim):
    return lax.broadcasted_iota(I32, shape, dim)


def one_hot(code, width):
    return jnp.where(iota((code.shape[0], width), 1) == code, 1.0, 0.0).astype(BF16)


def kernel(
    suffix, pages, placement, lengths, page_table, out,
    place_row, len_row, place_s, len_s, table, rows, heads_in, pool, pick, place, keys_in, vals_in, keys, vals, sent, got_0, got_1, got_2, got_3, got_kv, pairs_out, queries, mixed,
    ans_out, ans_in, ans, back,
    small_sem, rows_sem, pool_sem, x_send, x_recv, x_own, k_send, k_recv, k_own, f_send, f_recv, f_own,
    a_send, a_recv, a_own, b_send, b_recv, b_own,
):
    got = (got_0, got_1, got_2, got_3, got_kv)
    rep = lax.axis_index("rep")
    tp = lax.axis_index("tp")
    z, y = rep >> 3, rep & 7

    def peer(step):
        a, b = step >> 3, step & 7
        return (((z + b) & 7) << 3) + ((y + a + 3 * b) & 7)

    barrier = pltpu.get_barrier_semaphore()

    @pl.loop(1, REPS, unroll=REPS - 1)
    def _(step):
        pl.semaphore_signal(barrier, inc=1, device_id=(peer(step), tp), device_id_type=MESH)

    @pl.loop(1, TPS, unroll=TPS - 1)
    def _(step):
        pl.semaphore_signal(
            barrier, inc=1, device_id=(rep, (tp + step) & (TPS - 1)), device_id_type=MESH
        )

    rows_copy = pltpu.make_async_copy(suffix, rows, rows_sem)
    rows_copy.start()
    small = [
        pltpu.make_async_copy(source, target, small_sem.at[i])
        for i, (source, target) in enumerate(
            (
                (placement, place_row), (lengths, len_row),
                (placement, place_s), (lengths, len_s), (page_table, table),
            )
        )
    ]
    for copy in small:
        copy.start()
    pool_copy = pltpu.make_async_copy(pages, pool, pool_sem)
    pool_copy.start()

    def along_tp(copies, send, recv, own):
        @pl.loop(1, TPS)
        def _(step):
            to = (tp + step) & (TPS - 1)
            for source, target in copies(to):
                pltpu.make_async_remote_copy(
                    src_ref=source, dst_ref=target, send_sem=send, recv_sem=recv,
                    device_id=(rep, to), device_id_type=MESH,
                ).start()

        for source, target in copies(tp):
            pltpu.make_async_copy(source, target, own).start()

    def over_plane(source, target, send, recv, own):
        @pl.loop(1, REPS)
        def _(step):
            to = peer(step)
            pltpu.make_async_remote_copy(
                src_ref=source.at[to], dst_ref=target.at[rep], send_sem=send, recv_sem=recv,
                device_id=(to, tp), device_id_type=MESH,
            ).start()

        pltpu.make_async_copy(source.at[rep], target.at[rep], own).start()

    def wait_bytes(ref, count, sem):
        some = ref.at[pl.ds(0, count)]
        pltpu.make_async_copy(some, some, sem).wait()

    for copy in small:
        copy.wait()
    square = (REPS, REPS)
    lens_r = len_row[...].astype(F32)
    diagonal = iota(square, 0) == iota(square, 1)
    lens_c = jnp.sum(jnp.where(diagonal, lens_r, 0.0), axis=1, keepdims=True)
    starts_r = jnp.sum(
        jnp.where(iota(square, 0) < iota(square, 1), lens_c, 0.0), axis=0, keepdims=True
    )
    place_r = place_row[...]

    def round_of(start, order):
        return (start - order + (DEVICES - 1)) >> 9

    count = REPS * 2 * TPS
    row = iota((count, 1), 0)
    mine = place_r == iota((count, REPS), 0) >> 4
    start_g = jnp.sum(jnp.where(mine, starts_r, 0.0), axis=1, keepdims=True).astype(I32)
    round_g = round_of(start_g, rep * TPS + tp)
    code = jnp.where(round_g < ROUNDS, round_g + (row & (2 * TPS - 1)) * ROUNDS, -1)
    rows_copy.wait()
    pairs = jnp.concatenate(
        [rows[:, pl.ds((QUERY_HEADS + i) * HEAD, HEAD)] for i in range(2 * KEY_VALUE_HEADS)], axis=0
    )
    sent[KV] = (
        jnp.dot(one_hot(code, 2 * TPS * ROUNDS), pairs, preferred_element_type=F32)
        .astype(BF16)
        .reshape(REPS, 2 * TPS, HEAD)
    )

    pl.semaphore_wait(barrier, TPS - 1 + REPS - 1)

    def queries_along_tp(part):
        def copies(to):
            first = pl.multiple_of(to * (GROUP_HEADS * HEAD) + part * 2 * HEAD, HEAD)
            return ((rows.at[:, pl.ds(first, 2 * HEAD)], heads_in.at[part, tp]),)

        along_tp(copies, x_send.at[part], x_recv.at[part], x_own.at[part])

    queries_along_tp(0)
    over_plane(sent.at[KV], got[KV], f_send.at[KV], f_recv.at[KV], f_own.at[KV])
    for part in range(1, PARTS):
        queries_along_tp(part)

    run = iota((REPS * TPS, 1), 0) & (TPS - 1)
    mine = place_r == iota((REPS * TPS, REPS), 0) >> 3
    start_g = jnp.sum(jnp.where(mine, starts_r, 0.0), axis=1, keepdims=True).astype(I32)
    round_g = round_of(start_g, rep * TPS + run)
    pick[...] = one_hot(
        jnp.where(round_g < ROUNDS, round_g + run * ROUNDS, -1), TPS * ROUNDS
    )

    def chunk(part, half):
        tokens = heads_in[part, :, :, pl.ds(half * HEAD, HEAD)].reshape(TPS * ROUNDS, HEAD)
        return jnp.dot(pick[...], tokens, preferred_element_type=F32).reshape(REPS, TPS, HEAD)

    for part in range(PARTS):
        wait_bytes(heads_in.at[part], 1, x_own.at[part])
        wait_bytes(heads_in.at[part], TPS - 1, x_recv.at[part])
        sent[part] = jnp.concatenate([chunk(part, 0), chunk(part, 1)], axis=1).astype(BF16)
        over_plane(sent.at[part], got[part], f_send.at[part], f_recv.at[part], f_own.at[part])

    def wait_part(ref, recv, own):
        wait_bytes(ref, 1, own)
        wait_bytes(ref, REPS - 1, recv)

    turn = iota((256, 1), 0)
    turn = one_hot(((turn & 15) << 4) + (turn >> 4), 256)
    wait_part(got[KV], f_recv.at[KV], f_own.at[KV])
    for i in range(REPS // 16):
        block = got[KV][pl.ds(i * 16, 16)].reshape(256, HEAD)
        pairs_out[:, pl.ds(i * 16, 16)] = (
            jnp.dot(turn, block, preferred_element_type=F32).astype(BF16).reshape(16, 16, HEAD)
        )
    to_here = pl.ds(pl.multiple_of(tp * REPS, REPS), REPS)
    along_tp(
        lambda to: (
            (pairs_out.at[to], keys_in.at[to_here]),
            (pairs_out.at[TPS + to], vals_in.at[to_here]),
        ),
        k_send, k_recv, k_own,
    )

    place_c = jnp.sum(
        jnp.where(diagonal, place_r.astype(F32), 0.0), axis=1, keepdims=True
    ).astype(I32)
    starts_c = jnp.sum(
        jnp.where(iota(square, 1) < iota(square, 0), lens_r, 0.0), axis=1, keepdims=True
    )
    mine = place_c == iota((REPS, count), 1) >> 4
    start_l = jnp.sum(jnp.where(mine, starts_c, 0.0), axis=0, keepdims=True).astype(I32)
    length_l = jnp.sum(jnp.where(mine, lens_c, 0.0), axis=0, keepdims=True).astype(I32)
    order = rep * TPS + tp
    round_l = round_of(start_l, order)
    live = round_l * DEVICES + order < start_l + length_l
    code = round_l + ROUNDS * (iota((1, count), 1) & (2 * TPS - 1))
    shape = (2 * TPS * ROUNDS, count)
    place[...] = jnp.where(iota(shape, 0) == jnp.where(live, code, -1), 1.0, 0.0).astype(BF16)
    def add(r, carry):
        before, start = carry
        return before + len_s[0, r], start + jnp.where(place_s[0, r] == rep, before, 0)

    start = lax.fori_loop(0, REPS, add, (jnp.int32(0), jnp.int32(0)))[1]
    length = jnp.sum(jnp.where(place_r == rep, lens_r, 0.0), axis=1, keepdims=True).astype(I32)
    first_rep, shift = (start >> 3) & (REPS - 1), start & (TPS - 1)

    factor = math.log2(math.e) / math.sqrt(HEAD)

    def store_keys(first, block):
        scaled = block.astype(F32) * factor
        high = scaled.astype(BF16)
        keys[pl.ds(first, block.shape[0]), pl.ds(0, HEAD)] = high
        keys[pl.ds(first, block.shape[0]), pl.ds(HEAD, HEAD)] = (
            scaled - high.astype(F32)
        ).astype(BF16)

    pool_copy.wait()
    for i in range(PREFIX // HEAD):
        page = table[0, i]
        store_keys(i * HEAD, pool[0, page])
        vals[pl.ds(i * HEAD, HEAD)] = pool[1, page]
    mixed[...] = jnp.zeros_like(mixed)

    lane = iota((1, DEVICES), 1)
    pos = ((lane & (REPS - 1)) * TPS + (lane >> 6) - start) & (DEVICES - 1)
    pos = jnp.where(pos < length, pos, DEVICES)
    in_order = jnp.where(iota((LONGEST, DEVICES), 0) == pos, 1.0, 0.0).astype(BF16)
    wait_bytes(pairs_out, 2, k_own)
    wait_bytes(pairs_out, 2 * (TPS - 1), k_recv)
    store_keys(PREFIX, jnp.dot(in_order, keys_in[...], preferred_element_type=F32))
    vals[pl.ds(PREFIX, LONGEST)] = jnp.dot(
        in_order, vals_in[...], preferred_element_type=F32
    ).astype(BF16)

    tiles = BLOCK // (2 * TPS)
    index = iota((BLOCK, 1), 0)
    by_place = one_hot((((index >> 1) & 7) << 4) + ((index & 1) << 3) + (index >> 4), BLOCK)
    by_rep = one_hot((((index >> 1) & 7) << 4) + ((index >> 4) << 1) + (index & 1), BLOCK)

    def attend_runs(first, count, reach):
        height = count * 2 * TPS
        query = queries[pl.ds(first, count)].reshape(height, HEAD)
        row = iota((height, 1), 0)
        pos = (first + (row >> 4)) * TPS + (row & (TPS - 1)) - shift
        width = PREFIX + reach
        scores = lax.dot_general(
            jnp.concatenate([query, query], axis=1), keys[pl.ds(0, width)],
            (((1,), (1,)), ((), ())), preferred_element_type=F32,
        )
        seen = PREFIX + max(0, (first * TPS - TPS) // HEAD * HEAD)
        column = iota((1, width - seen), 1) + (seen - PREFIX)
        after = jnp.where(column <= pos, scores[:, seen:], -jnp.inf)
        scores = jnp.concatenate([scores[:, :seen], after], axis=1)
        expo = jnp.exp2(scores - jnp.max(scores, axis=1, keepdims=True))
        total = jnp.sum(expo, axis=1, keepdims=True)
        result = jnp.dot(expo.astype(BF16), vals[pl.ds(0, width)], preferred_element_type=F32)
        mixed[pl.ds(first, count)] = (result / total).astype(BF16).reshape(count, 2 * TPS, HEAD)

    def arrive(part):
        wait_part(got[part], f_recv.at[part], f_own.at[part])

    def attend(part):
        for run in range(RUNS):
            queries[run] = got[part][(first_rep + run) & (REPS - 1)]
        step = HEAD // TPS
        for i in range(LONGEST // HEAD):
            last = i == LONGEST // HEAD - 1
            attend_runs(i * step, step + (RUNS - LONGEST // TPS if last else 0), (i + 1) * HEAD)
        for i in range(REPS // tiles):
            block = [mixed[(i * tiles + m - first_rep) & (REPS - 1)] for m in range(tiles)]
            block = jnp.dot(by_place, jnp.concatenate(block, axis=0), preferred_element_type=F32)
            ans_out[part, :, pl.ds(i * 2 * tiles, 2 * tiles)] = block.astype(BF16).reshape(
                TPS, 2 * tiles, HEAD
            )
        along_tp(
            lambda to: ((ans_out.at[part, to], ans_in.at[part, tp]),),
            a_send.at[part], a_recv.at[part], a_own.at[part],
        )

    def prepare(part):
        wait_bytes(ans_in.at[part], 1, a_own.at[part])
        wait_bytes(ans_in.at[part], TPS - 1, a_recv.at[part])
        for i in range(REPS // tiles):
            block = ans_in[part, :, pl.ds(i * 2 * tiles, 2 * tiles)].reshape(BLOCK, HEAD)
            ans[part, pl.ds(i * tiles, tiles)] = (
                jnp.dot(by_rep, block, preferred_element_type=F32)
                .astype(BF16)
                .reshape(tiles, 2 * TPS, HEAD)
            )

    def answer(part):
        over_plane(ans.at[part], back.at[part], b_send.at[part], b_recv.at[part], b_own.at[part])

    arrive(0)
    attend(0)
    arrive(1)
    attend(1)
    prepare(0)
    answer(0)
    arrive(2)
    attend(2)
    prepare(1)
    answer(1)
    arrive(3)
    attend(3)
    prepare(2)
    answer(2)
    prepare(3)
    answer(3)

    for part in range(PARTS):
        wait_part(back.at[part], b_recv.at[part], b_own.at[part])
        tokens = jnp.dot(
            place[...], back[part].reshape(count, HEAD), preferred_element_type=F32
        ).astype(BF16).reshape(TPS, 2, ROUNDS, HEAD)
        for head in range(TPS):
            for half in range(2):
                column = (head * GROUP_HEADS + 2 * part + half) * HEAD
                out[:, pl.ds(column, HEAD)] = tokens[head, half]
    for part in range(PARTS):
        wait_bytes(heads_in.at[part], TPS - 1, x_send.at[part])
        wait_bytes(ans_out.at[part], TPS - 1, a_send.at[part])
        wait_bytes(ans.at[part], REPS - 1, b_send.at[part])
    for part in range(PARTS + 1):
        wait_bytes(sent.at[part], REPS - 1, f_send.at[part])
    wait_bytes(pairs_out, 2 * (TPS - 1), k_send)


def shards(suffix, key_value_pages, placement, lengths, page_table):
    message = (REPS, 2 * TPS, HEAD)
    dma = pltpu.SemaphoreType.DMA
    parts = dma((PARTS,))
    anywhere = pl.BlockSpec(memory_space=pl.ANY)
    return pl.pallas_call(
        kernel,
        out_shape=jax.ShapeDtypeStruct((ROUNDS, QUERY_HEADS * HEAD), BF16),
        in_specs=[anywhere] * 5,
        out_specs=pl.BlockSpec(memory_space=pltpu.VMEM),
        scratch_shapes=[
            pltpu.VMEM((1, REPS), I32),
            pltpu.VMEM((1, REPS), I32),
            pltpu.SMEM((1, REPS), I32),
            pltpu.SMEM((1, REPS), I32),
            pltpu.SMEM(page_table.shape, I32),
            pltpu.VMEM(suffix.shape, BF16),
            pltpu.VMEM((PARTS, TPS, ROUNDS, 2 * HEAD), BF16),
            pltpu.VMEM(key_value_pages.shape, BF16),
            pltpu.VMEM((REPS * TPS, TPS * ROUNDS), BF16),
            pltpu.VMEM((2 * TPS * ROUNDS, 2 * REPS * TPS), BF16),
            pltpu.VMEM((DEVICES, HEAD), BF16),
            pltpu.VMEM((DEVICES, HEAD), BF16),
            pltpu.VMEM((PREFIX + LONGEST, 2 * HEAD), BF16),
            pltpu.VMEM((PREFIX + LONGEST, HEAD), BF16),
            pltpu.VMEM((PARTS + 1, *message), BF16),
            *[pltpu.VMEM(message, BF16)] * (PARTS + 1),
            pltpu.VMEM((2 * TPS, REPS, HEAD), BF16),
            pltpu.VMEM((RUNS, 2 * TPS, HEAD), BF16),
            pltpu.VMEM(message, BF16),
            pltpu.VMEM((PARTS, TPS, 2 * REPS, HEAD), BF16),
            pltpu.VMEM((PARTS, TPS, 2 * REPS, HEAD), BF16),
            pltpu.VMEM((PARTS, *message), BF16),
            pltpu.VMEM((PARTS, *message), BF16),
            dma((5,)), dma, dma,
            parts, parts, parts,
            dma, dma, dma,
            dma((PARTS + 1,)), dma((PARTS + 1,)), dma((PARTS + 1,)),
            parts, parts, parts,
            parts, parts, parts,
        ],
        compiler_params=pltpu.CompilerParams(
            collective_id=0, has_side_effects=True, vmem_limit_bytes=56_100_000
        ),
        cost_estimate=pl.CostEstimate(
            flops=4 * 4096 * 1024 * HEAD, bytes_accessed=2**20, transcendentals=4096 * 1024
        ),
    )(
        suffix,
        key_value_pages,
        placement.reshape(1, REPS),
        lengths.reshape(1, REPS),
        page_table,
    )


def solution(mesh):
    return jax.shard_map(
        shards,
        mesh=mesh,
        in_specs=(P(("rep", "tp"), None), P(None, "rep", None, "tp"), P(), P(), P("rep", None)),
        out_specs=P(("rep", "tp"), None),
        check_vma=False,
    )
```
